128 devices in a mesh: dp: 16 (over z_hi, y, core), blk: 8 (over x, z_lo).
Axes of the slice: x: 4, y: 4, z: 4 (z_hi: 2, z_lo: 2; z = z_hi * 2 + z_lo), core: 2. Of those that a mesh axis runs over, the one named last changes fastest.
Arguments:
- teacher_image: bfloat16 [16384, 1152], P(('dp', 'blk')), may hold values from -7 to 7
- teacher_text: bfloat16 [16384, 1152], P(('dp', 'blk')), may hold values from -7 to 7
- student_image: bfloat16 [16384, 768], P(('dp', 'blk')), may hold values from -0.21875 to 0.21875
- student_text: bfloat16 [16384, 768], P(('dp', 'blk')), may hold values from -0.21875 to 0.21875
Outputs:
- image_grad: float32 [16384, 768], P(('dp', 'blk'))
- text_grad: float32 [16384, 768], P(('dp', 'blk'))
- kd_loss: float32 [], replicated
The draws below stay inside these ranges and needn't reach their ends.
All inputs are finite; a program needn't handle non-finite values.
Results may differ from the reference program's by a relative error of at most 0.0045.
Values may be sent and summed in bfloat16 or wider, within the bound.
No kernel may reach another device: no remote copies, remote signals or barrier semaphores. Data moves between devices by JAX's collectives and lax.ppermute only.
A program may use at most 64 MiB of HBM per device.

```python
import jax
import jax.numpy as jnp
from jax import lax

D_T = 1152
D_S = 768
B_DEV = 128
PAIRS = 16384


def common_signs(key):
    bits = jax.random.bernoulli(jax.random.fold_in(key, 101), 0.5, (D_T,))
    return jnp.where(bits, 1.0, -1.0).astype(jnp.float32)


def teacher_rows(signs, power, noise):
    place = jnp.arange(PAIRS, dtype=jnp.float32) / float(PAIRS)
    strength = place ** power
    return noise + strength[:, None] * signs[None, :]


def draw_teacher_image(key, part):
    signs = common_signs(key)
    key = jax.random.fold_in(key, 7)
    noise = jax.random.truncated_normal(key, -5.5, 5.5, (PAIRS, D_T), jnp.float32)
    rows = teacher_rows(signs, 1.0, noise)
    return rows.astype(jnp.bfloat16)


def draw_teacher_text(key, part):
    signs = common_signs(key)
    key = jax.random.fold_in(key, 13)
    noise = jax.random.truncated_normal(key, -5.5, 5.5, (PAIRS, D_T), jnp.float32)
    rows = teacher_rows(signs, 1.0, noise)
    return rows.astype(jnp.bfloat16)


def level_of(own_key, dims, split, least, top_value):
    loudness, own = 1.0, jax.random.fold_in(own_key, 6)
    for axis_at, parts in split:
        draws = jnp.exp(jax.random.uniform(jax.random.fold_in(own, axis_at), (parts,), jnp.float32, least / len(split), top_value / len(split)))
        loudness = loudness * jnp.repeat(draws, dims[axis_at] // parts).reshape([-1 if axis == axis_at else 1 for axis in range(len(dims))])
    return loudness


def bell_draw(key, shape, width, most, split=(), kind=jnp.bfloat16):
    gain = level_of(key, shape, split, -0.22, 0.18) if split else 1.0
    values = jax.random.normal(key, shape, jnp.float32) * width * gain
    return jnp.minimum(jnp.maximum(values, -most), most).astype(kind)


def setup_inputs(seed: int = 0) -> dict:
    key_of = jax.random.split(jax.random.key(seed), 5)
    teacher_image = draw_teacher_image(jax.random.fold_in(key_of[4], 71), 0)
    teacher_text = draw_teacher_text(jax.random.fold_in(key_of[4], 71), 0)
    student_image = bell_draw(key_of[2], (PAIRS, D_S), D_S ** -0.5, 0.21875, ((0, 128),))
    student_text = bell_draw(key_of[3], (PAIRS, D_S), D_S ** -0.5, 0.21875, ((0, 128),))
    return {"teacher_image": teacher_image, "teacher_text": teacher_text, "student_image": student_image, "student_text": student_text}


eps = 1e-06
scale_t = 10.0
bias_t = -2.0
scale_s = 10.0
bias_s = -2.0

def unit_rows(values):
    wide = values.astype(jnp.float32)
    norms = jnp.sqrt(lax.optimization_barrier(jnp.sum(wide * wide, axis=-1, keepdims=True)) + eps)
    return (wide / norms, norms)

def reference(teacher_image, teacher_text, student_image, student_text):
    teach_img = unit_rows(teacher_image)[0].astype(jnp.bfloat16)
    teach_txt = unit_rows(teacher_text)[0].astype(jnp.bfloat16)
    unit_img, norm_img = unit_rows(student_image)
    unit_txt, norm_txt = unit_rows(student_text)
    stud_img = unit_img.astype(jnp.bfloat16)
    stud_txt = unit_txt.astype(jnp.bfloat16)
    blocks = PAIRS // B_DEV
    img_blocks = (teach_img.reshape(blocks, B_DEV, D_T), stud_img.reshape(blocks, B_DEV, D_S))

    def step(running, block):
        loss_sum, text_acc = running
        block_t, block_s = block
        teach_logit = jnp.dot(block_t, teach_txt.T, preferred_element_type=jnp.float32) * scale_t + bias_t
        target = jax.nn.sigmoid(teach_logit)
        stud_logit = jnp.dot(block_s, stud_txt.T, preferred_element_type=jnp.float32) * scale_s + bias_s
        loss_sum = loss_sum + jnp.sum(jax.nn.softplus(stud_logit) - target * stud_logit)
        coef = ((jax.nn.sigmoid(stud_logit) - target) * scale_s).astype(jnp.bfloat16)
        img_part = jnp.dot(coef, stud_txt, preferred_element_type=jnp.float32)
        text_acc = text_acc + jnp.dot(coef.T, block_s, preferred_element_type=jnp.float32)
        return ((loss_sum, text_acc), img_part)
    init = (jnp.zeros((), jnp.float32), jnp.zeros((PAIRS, D_S), jnp.float32))
    (loss_sum, grad_txt), img_parts = lax.scan(step, init, img_blocks)
    grad_img = img_parts.reshape(PAIRS, D_S)
    image_grad = (grad_img - lax.optimization_barrier(jnp.sum(grad_img * unit_img, axis=-1, keepdims=True)) * unit_img) / norm_img
    text_grad = (grad_txt - lax.optimization_barrier(jnp.sum(grad_txt * unit_txt, axis=-1, keepdims=True)) * unit_txt) / norm_txt
    kd_loss = loss_sum / (float(PAIRS) * float(PAIRS))
    return (image_grad, text_grad, kd_loss)
```

```python
import functools
import itertools

import jax
import jax.numpy as jnp
from jax import lax
from jax.experimental import pallas as pl
from jax.experimental.pallas import tpu as pltpu
from jax.sharding import PartitionSpec as P

eps = 1e-06
scale = 10.0
bias = -2.0
AXES = ("dp", "blk")
f32, bf16 = jnp.float32, jnp.bfloat16

ZH, Y, C, X, ZL = 2, 4, 2, 4, 2
NT = (((1,), (1,)), ((), ()))
TN = (((0,), (0,)), ((), ()))


def place(zh, y, c, x, zl):
    return ((zh * Y + y) * C + c) * (X * ZL) + x * ZL + zl


def permute(value, move):
    pairs = [
        (place(*at), place(*move(*at)))
        for at in itertools.product(range(ZH), range(Y), range(C), range(X), range(ZL))
    ]
    return lax.ppermute(value, AXES, pairs)


def to_x(value, step):
    return permute(value, lambda zh, y, c, x, zl: (zh, y, c, (x + step) % X, zl))


def to_y(value, step):
    return permute(value, lambda zh, y, c, x, zl: (zh, (y + step) % Y, c, x, zl))


def flip_x(value, bits):
    return permute(value, lambda zh, y, c, x, zl: (zh, y, c, x ^ bits, zl))


def flip_y(value, bits):
    return permute(value, lambda zh, y, c, x, zl: (zh, y ^ bits, c, x, zl))


def to_core(value):
    return permute(value, lambda zh, y, c, x, zl: (zh, y, 1 - c, x, zl))


def to_image_z(value):
    return permute(value, lambda zh, y, c, x, zl: (zh, y, c, x, 1 - zl))


def to_text_z(value):
    return permute(value, lambda zh, y, c, x, zl: (1 - zh, y, c, x, 1 - zl))


def to_far_z(value):
    return permute(value, lambda zh, y, c, x, zl: (1 - zh, y, c, x, zl))


def call(kernel, name, args, outs, limit=16, far=(), keep=True, flops=0, scratch=()):
    vmem = pl.BlockSpec(memory_space=pltpu.VMEM)
    near = [
        pltpu.with_memory_space_constraint(v, pltpu.HBM if any(v is w for w in far) else pltpu.VMEM) for v in args
    ]
    shape_of = pltpu.VMEM if keep else jax.ShapeDtypeStruct
    return pl.pallas_call(
        kernel,
        out_shape=tuple(shape_of(shape, dtype) for shape, dtype in outs),
        in_specs=[vmem] * len(args),
        out_specs=(vmem,) * len(outs),
        scratch_shapes=[pltpu.VMEM(shape, dtype) for shape, dtype in scratch],
        compiler_params=pltpu.CompilerParams(vmem_limit_bytes=limit * 2**20),
        cost_estimate=pl.CostEstimate(
            flops=flops, transcendentals=0, bytes_accessed=sum(v.size * v.dtype.itemsize for v in args),
        ),
        name=name,
    )(*near)


def norm_of(wide):
    return jnp.sqrt(jnp.sum(wide * wide, axis=-1, keepdims=True) + eps)


def units_kernel(ti, si, tt, st, img, txt):
    for teach, stud, out in ((ti, si, img), (tt, st, txt)):
        wide = teach[...].astype(f32)
        split = wide.shape[1]
        out[:, :split] = (wide / norm_of(wide)).astype(bf16)
        wide = stud[...].astype(f32)
        out[:, split:] = (wide / norm_of(wide)).astype(bf16)


def tile_terms(cos_t, cos_s):
    half_s = cos_s * (0.5 * scale) + 0.5 * bias
    tanh_t = jnp.tanh(cos_t * (0.5 * scale) + 0.5 * bias)
    tanh_s = jnp.tanh(half_s)
    coef = ((tanh_s - tanh_t) * (0.5 * scale)).astype(bf16)
    left = 1.0 - tanh_s
    for _ in range(3):
        rows = left.shape[0] // 2
        left = left[:rows] * left[rows:]
    line = half_s + half_s * tanh_t
    fold = lambda v: jnp.sum(v.reshape(-1, 8, v.shape[1]), axis=0)
    loss = -(fold(jnp.log(left)) + fold(line))
    return coef, sum(loss[:, k:k + 128] for k in range(0, loss.shape[1], 128))


def stack(refs, cols):
    return jnp.concatenate([r[:, cols] for r in refs], axis=0)


def dot(a, b, dims=(((1,), (0,)), ((), ()))):
    return lax.dot_general(a, b, dims, preferred_element_type=f32)


def near_tile_kernel(width_t, *refs):
    imgs, txt, oth, (g_img, g_txt, g_oth, loss_ref) = refs[:3], refs[3:6], refs[6:9], refs[9:]
    cols_t, cols_s = slice(0, width_t), slice(width_t, None)
    img_t, img_s = stack(imgs, cols_t), stack(imgs, cols_s)
    text_s = stack(list(txt) + list(oth), cols_s)
    coef, loss = tile_terms(dot(img_t, stack(list(txt) + list(oth), cols_t), NT), dot(img_s, text_s, NT))
    loss_ref[...] = loss
    g_img[...] = dot(coef, text_s)
    half = g_txt.shape[0]
    g_txt[...] = dot(coef[:, :half], img_s, TN)
    g_oth[...] = dot(coef[:, half:], img_s, TN)


def first_tile_kernel(width_t, *refs):
    imgs, txt, oth, refs = refs[:5], refs[5:10], refs[10:15], refs[15:]
    p_img, p_txt, p_oth, p_loss, g_img, g_txt, g_oth, loss_ref, coef_n, coef_f = refs
    cols_t, cols_s = slice(0, width_t), slice(width_t, None)
    own, zed, left, right, far = range(5)
    near = [[txt[own], txt[zed]], [oth[own], oth[zed]], [txt[left], oth[left]]]
    wide = [[txt[right]], [txt[far]], [oth[right]], [oth[far]]]
    total = p_loss[...]
    img_t, img_s = stack(imgs, cols_t), stack(imgs, cols_s)
    far_t, far_s = stack(imgs[3:], cols_t), stack(imgs[3:], cols_s)
    for n, texts in enumerate(wide):
        part, loss = tile_terms(dot(img_t, stack(texts, cols_t), NT), dot(img_s, stack(texts, cols_s), NT))
        coef_f[:, n * 256:(n + 1) * 256] = part
        total = total + loss
    for n, texts in enumerate(near):
        part, loss = tile_terms(dot(far_t, stack(texts, cols_t), NT), dot(far_s, stack(texts, cols_s), NT))
        coef_n[:, n * 256:(n + 1) * 256] = part
        total = total + loss
    loss_ref[...] = total
    wide_s = jnp.concatenate([stack(texts, cols_s) for texts in wide], axis=0)
    near_s = jnp.concatenate([stack(texts, cols_s) for texts in near], axis=0)
    g_img[0:384, :] = p_img[...] + dot(coef_f[0:384, :], wide_s)
    g_img[384:, :] = dot(coef_f[384:, :], wide_s) + dot(coef_n[...], near_s)
    for n, (ref, row) in enumerate([(g_txt, 384), (g_txt, 640), (g_oth, 384), (g_oth, 640)]):
        ref[row:row + 256, :] = dot(coef_f[:, n * 256:(n + 1) * 256], img_s, TN)
    g_txt[0:256, :] = p_txt[0:256, :] + dot(coef_n[:, 0:256], far_s, TN)
    g_oth[0:256, :] = p_oth[0:256, :] + dot(coef_n[:, 256:512], far_s, TN)
    grad = dot(coef_n[:, 512:768], far_s, TN)
    g_txt[256:384, :] = p_txt[256:, :] + grad[:128]
    g_oth[256:384, :] = p_oth[256:, :] + grad[128:]


def last_coef_kernel(width_t, *refs):
    imgs, texts, (p_loss, coef_a, coef_b, loss_ref) = refs[:6], refs[6:18], refs[18:]
    cols_t, cols_s = slice(0, width_t), slice(width_t, None)
    last_i, last_t = imgs[5], [texts[5], texts[11]]
    part_a, loss_a = tile_terms(
        dot(stack(texts, cols_t), last_i[:, cols_t], NT), dot(stack(texts, cols_s), last_i[:, cols_s], NT)
    )
    part_b, loss_b = tile_terms(
        dot(stack(imgs[:5], cols_t), stack(last_t, cols_t), NT), dot(stack(imgs[:5], cols_s), stack(last_t, cols_s), NT)
    )
    coef_a[...] = part_a
    coef_b[...] = part_b
    loss_ref[...] = p_loss[...] + loss_a + loss_b


def other_grad_kernel(width_t, *refs):
    imgs, (coef_a, coef_b, part, out) = refs[:6], refs[6:]
    most = part.shape[0]
    grad = dot(coef_a[most + 128:, :], imgs[5][:, width_t:])
    out[:most, :] = (part[...] + grad[:most]).astype(bf16)
    last = dot(coef_b[:, 128:], stack(imgs[:5], slice(width_t, None)), TN)
    out[most:, :] = (grad[most:] + last).astype(bf16)


def text_grad_kernel(width_t, *refs):
    imgs, (coef_a, coef_b, part, from_core, t0, t1, t2, t3, t4) = refs[:6], refs[6:]
    most = part.shape[0]
    grad = dot(coef_a[:most + 128, :], imgs[5][:, width_t:]) + from_core[...].astype(f32)
    last = dot(coef_b[:, :128], stack(imgs[:5], slice(width_t, None)), TN)
    at = lambda low, high: part[low:high, :] + grad[low:high]
    t0[...] = at(0, 256)
    t1[0:128, :] = at(256, 384).astype(bf16)
    t1[128:256, :] = at(640, 768).astype(bf16)
    t2[...] = at(384, 640).astype(bf16)
    t3[...] = at(768, 896)
    t4[...] = (grad[most:] + last).astype(bf16)


def image_grad_kernel(width_t, *refs):
    texts, (coef_a, coef_b, part, loss, i0, i1, i2, i3, i4) = refs[:12], refs[12:]
    cols_s = slice(width_t, None)
    grad = part[...] + dot(coef_b[...], stack([texts[5], texts[11]], cols_s))
    i0[...] = grad[0:256]
    i1[0:128, :] = grad[256:384].astype(bf16)
    i1[128:256, :] = grad[640:768].astype(bf16)
    i2[0:256, :] = grad[384:640].astype(bf16)
    i3[...] = grad[768:896]
    i4[...] = dot(coef_a[...], stack(texts, cols_s), TN).astype(bf16)
    for ref in (i1, i2):
        put_pieces(ref, 256, loss[...])


def join(*parts):
    return jnp.concatenate(parts, axis=0)


def put_pieces(ref, row, value):
    ref[row:row + 16, :] = jnp.zeros((16, ref.shape[1]), bf16)
    first = value.astype(bf16)
    second = (value - first.astype(f32)).astype(bf16)
    third = (value - first.astype(f32) - second.astype(f32)).astype(bf16)
    ref[row:row + 16, 0:128] = jnp.concatenate([first, first], axis=0)
    ref[row:row + 16, 128:256] = jnp.concatenate([second, second], axis=0)
    ref[row:row + 16, 256:384] = jnp.concatenate([third, third], axis=0)


def get_pieces(ref, row):
    at = lambda k: ref[row:row + 16, k:k + 128].astype(f32)[:8]
    return at(0) + at(128) + at(256)


def ring_sum_kernel(*refs):
    ins, (loss, loss_x), outs = refs[:10], refs[10:12], refs[12:]
    total_loss = loss[...] + loss_x[...] + get_pieces(ins[6], 256) + get_pieces(ins[7], 256)
    outs[6][...] = total_loss
    for n in range(2):
        (own, one, two, far, from_z), (near, to_z, to_far) = ins[5 * n:5 * n + 5], outs[3 * n:3 * n + 3]
        rows = near.shape[0]
        total = own[...] + one[:2 * rows, :].astype(f32) + two[:2 * rows, :].astype(f32)
        near[...] = total[:rows]
        to_z[:rows, :] = total[rows:].astype(bf16)
        put_pieces(to_z, rows, total_loss)
        to_far[...] = (far[...] + from_z[...].astype(f32)).astype(bf16)


def finish_kernel(
    scale_loss, loss, loss_far, txt, txt_z, txt_x, img, img_z, img_x, si, st, img_out, txt_out, loss_out
):
    rows = txt.shape[0]
    for stud, near, far, ring, out in ((si, img, img_z, img_x, img_out), (st, txt, txt_z, txt_x, txt_out)):
        wide = stud[...].astype(f32)
        norm = norm_of(wide)
        unit = wide / norm
        grad = near[...] + far[:rows, :].astype(f32) + ring[...].astype(f32)
        out[...] = (grad - jnp.sum(grad * unit, axis=-1, keepdims=True) * unit) / norm
    total = (loss[...] + loss_far[...]) + (get_pieces(img_z, rows) + get_pieces(txt_z, rows))
    loss_out[...] = jnp.sum(total, keepdims=True) * scale_loss + jnp.log(2.0)


def body(teacher_image, teacher_text, student_image, student_text):
    rows, width_t = teacher_image.shape
    width_s = student_image.shape[1]
    width = width_t + width_s
    img, txt = call(
        units_kernel, "units", (teacher_image, student_image, teacher_text, student_text),
        [((rows, width), bf16)] * 2,
        far=(teacher_image, student_image, teacher_text, student_text),
    )

    hold = lax.optimization_barrier
    txt_z, img_z, txt_l, img_l = hold((to_text_z(txt), to_image_z(img), to_y(txt, 1), to_x(img, 1)))
    core_1 = to_core(join(txt, txt_z, txt_l))
    txt_r, img_r = to_y(join(txt, txt_z), -1), to_x(join(img, img_z), -1)
    txt_q, img_q = to_y(join(txt_z, txt_l), 1), to_x(join(img_z, img_l), 1)
    imgs, own = [img, img_z, img_l], [txt, txt_z, txt_l]
    other = [core_1[n * rows:(n + 1) * rows] for n in range(3)]
    most, some = 7 * rows, 3 * rows
    near = call(
        functools.partial(near_tile_kernel, width_t), "near_tile", (*imgs, *own, *other),
        [((some, width_s), f32)] * 3 + [((8, 128), f32)],
        flops=2 * some * 2 * some * (width + 2 * width_s),
    )
    txt_r, img_r, txt_q, img_q, near_loss = hold((txt_r, img_r, txt_q, img_q, near[3]))
    near = [*near[:3], near_loss]
    cut = rows // 2
    core_2 = to_core(join(txt_r, txt_q))
    txt_h = [to_y(txt_q[:cut], 1), to_y(txt_r[-cut:], -1)]
    img_h = [to_x(img_q[:cut], 1), to_x(img_r[-cut:], -1)]
    imgs += [img_r, img_q]
    own += [txt_r, txt_q]
    other += [core_2[:2 * rows], core_2[2 * rows:]]
    p_img, p_txt, p_oth, p_loss = call(
        functools.partial(first_tile_kernel, width_t), "first_tile", (*imgs, *own, *other, *near),
        [((most, width_s), f32)] * 3 + [((8, 128), f32)], limit=24,
        flops=2 * (most * 2 * most - some * 2 * some) * (width + 2 * width_s),
        scratch=[((4 * rows, 6 * rows), bf16), ((most, 8 * rows), bf16)],
    )
    txt_h, img_h, p_loss = hold((txt_h, img_h, p_loss))
    txt_h, img_h = join(*txt_h), join(*img_h)
    core_3 = to_core(txt_h)
    pair = 2 * rows
    imgs, texts = [*imgs, img_h], [*own, txt_h, *other, core_3]
    work = 2 * 2 * most * rows
    coef_a, coef_b, loss = call(
        functools.partial(last_coef_kernel, width_t), "last_coef", (*imgs, *texts, p_loss),
        [((2 * (most + rows), rows), bf16), ((most, pair), bf16), ((8, 128), f32)], flops=2 * work * width,
    )
    loss = loss + to_core(loss)
    grad_o = call(
        functools.partial(other_grad_kernel, width_t), "other_grad", (*imgs, coef_a, coef_b, p_oth),
        [((most + rows, width_s), bf16)], flops=work * width_s,
    )[0]
    from_core = to_core(grad_o)
    loss = loss + to_y(loss, 1) + to_y(loss, -1) + to_y(loss, 2)
    sums = [((rows, width_s), f32), ((rows, width_s), bf16)]
    t0, t1, t2, t3, t4 = call(
        functools.partial(text_grad_kernel, width_t), "text_grad", (*imgs, coef_a, coef_b, p_txt, from_core),
        [((pair, width_s), f32)] + [((pair, width_s), bf16)] * 2 + sums, flops=work * width_s,
    )
    i0, i1, i2, i3, i4 = call(
        functools.partial(image_grad_kernel, width_t), "image_grad", (*texts, coef_a, coef_b, p_img, loss),
        [((pair, width_s), f32)] + [((pair + 16, width_s), bf16)] * 2 + sums, flops=2 * work * width_s,
    )
    t1, t2, t4 = to_y(t1, -1), to_y(t2, 1), to_text_z(t4)
    i1, i2, i4 = to_x(i1, -1), to_x(i2, 1), to_image_z(i4)
    loss_x = to_x(loss, 2)
    txt, txt_z, txt_x, img, img_z, img_x, loss = call(
        ring_sum_kernel, "ring_sum", (t0, t1, t2, t3, t4, i0, i1, i2, i3, i4, loss, loss_x),
        [((rows, width_s), f32), ((rows + 16, width_s), bf16), ((rows, width_s), bf16)] * 2 + [((8, 128), f32)],
    )
    txt_x, img_x = to_y(txt_x, 2), to_x(img_x, 2)
    txt_z, img_z, loss_far = to_text_z(txt_z), to_image_z(img_z), to_far_z(loss)
    pairs = float(rows * lax.axis_size("dp") * lax.axis_size("blk"))
    image_grad, text_grad, loss = call(
        functools.partial(finish_kernel, 1.0 / (pairs * pairs)), "finish",
        (loss, loss_far, txt, txt_z, txt_x, img, img_z, img_x, student_image, student_text),
        [((rows, width_s), f32)] * 2 + [((1, 1), f32)],
        keep=False,
    )
    return (image_grad, text_grad, loss.reshape(()))


def solution(mesh):
    spec = P(AXES, None)
    return jax.shard_map(body, mesh=mesh, in_specs=(spec,) * 4, out_specs=(spec, spec, P()), check_vma=False)
```

```python
import functools
import itertools

import jax
import jax.numpy as jnp
from jax import lax
from jax.experimental import pallas as pl
from jax.experimental.pallas import tpu as pltpu
from jax.sharding import PartitionSpec as P

eps = 1e-06
scale = 10.0
bias = -2.0
AXES = ("dp", "blk")
f32, bf16 = jnp.float32, jnp.bfloat16

ZH, Y, C, X, ZL = 2, 4, 2, 4, 2
NT = (((1,), (1,)), ((), ()))
TN = (((0,), (0,)), ((), ()))


def place(zh, y, c, x, zl):
    return ((zh * Y + y) * C + c) * (X * ZL) + x * ZL + zl


def permute(value, move):
    pairs = [
        (place(*at), place(*move(*at)))
        for at in itertools.product(range(ZH), range(Y), range(C), range(X), range(ZL))
    ]
    return lax.ppermute(value, AXES, pairs)


def to_x(value, step):
    return permute(value, lambda zh, y, c, x, zl: (zh, y, c, (x + step) % X, zl))


def to_y(value, step):
    return permute(value, lambda zh, y, c, x, zl: (zh, (y + step) % Y, c, x, zl))


def flip_x(value, bits):
    return permute(value, lambda zh, y, c, x, zl: (zh, y, c, x ^ bits, zl))


def flip_y(value, bits):
    return permute(value, lambda zh, y, c, x, zl: (zh, y ^ bits, c, x, zl))


def to_core(value):
    return permute(value, lambda zh, y, c, x, zl: (zh, y, 1 - c, x, zl))


def to_image_z(value):
    return permute(value, lambda zh, y, c, x, zl: (zh, y, c, x, 1 - zl))


def to_text_z(value):
    return permute(value, lambda zh, y, c, x, zl: (1 - zh, y, c, x, 1 - zl))


def to_far_z(value):
    return permute(value, lambda zh, y, c, x, zl: (1 - zh, y, c, x, zl))


def call(kernel, name, args, outs, limit=16, far=(), keep=True, flops=0, scratch=()):
    vmem = pl.BlockSpec(memory_space=pltpu.VMEM)
    near = [
        pltpu.with_memory_space_constraint(v, pltpu.HBM if any(v is w for w in far) else pltpu.VMEM) for v in args
    ]
    shape_of = pltpu.VMEM if keep else jax.ShapeDtypeStruct
    return pl.pallas_call(
        kernel,
        out_shape=tuple(shape_of(shape, dtype) for shape, dtype in outs),
        in_specs=[vmem] * len(args),
        out_specs=(vmem,) * len(outs),
        scratch_shapes=[pltpu.VMEM(shape, dtype) for shape, dtype in scratch],
        compiler_params=pltpu.CompilerParams(vmem_limit_bytes=limit * 2**20),
        cost_estimate=pl.CostEstimate(
            flops=flops, transcendentals=0, bytes_accessed=sum(v.size * v.dtype.itemsize for v in args),
        ),
        name=name,
    )(*near)


def norm_of(wide):
    return jnp.sqrt(jnp.sum(wide * wide, axis=-1, keepdims=True) + eps)


def units_kernel(ti, si, tt, st, img, txt):
    for teach, stud, out in ((ti, si, img), (tt, st, txt)):
        wide = teach[...].astype(f32)
        split = wide.shape[1]
        out[:, :split] = (wide / norm_of(wide)).astype(bf16)
        wide = stud[...].astype(f32)
        out[:, split:] = (wide / norm_of(wide)).astype(bf16)


def tile_terms(cos_t, cos_s):
    half_s = cos_s * (0.5 * scale) + 0.5 * bias
    tanh_t = jnp.tanh(cos_t * (0.5 * scale) + 0.5 * bias)
    tanh_s = jnp.tanh(half_s)
    coef = ((tanh_s - tanh_t) * (0.5 * scale)).astype(bf16)
    left = 1.0 - tanh_s
    for _ in range(3):
        rows = left.shape[0] // 2
        left = left[:rows] * left[rows:]
    line = half_s + half_s * tanh_t
    fold = lambda v: jnp.sum(v.reshape(-1, 8, v.shape[1]), axis=0)
    loss = -(fold(jnp.log(left)) + fold(line))
    return coef, sum(loss[:, k:k + 128] for k in range(0, loss.shape[1], 128))


def stack(refs, cols):
    return jnp.concatenate([r[:, cols] for r in refs], axis=0)


def dot(a, b, dims=(((1,), (0,)), ((), ()))):
    return lax.dot_general(a, b, dims, preferred_element_type=f32)


def near_tile_kernel(width_t, *refs):
    imgs, texts, (g_img, g_txt, g_oth, loss_ref) = refs[:3], refs[3:5], refs[5:]
    cols_t, cols_s = slice(0, width_t), slice(width_t, None)
    img_t, img_s, text_s = stack(imgs, cols_t), stack(imgs, cols_s), stack(texts, cols_s)
    coef, loss = tile_terms(dot(img_t, stack(texts, cols_t), NT), dot(img_s, text_s, NT))
    loss_ref[...] = loss
    g_img[...] = dot(coef, text_s)
    half = g_txt.shape[0]
    g_txt[...] = dot(coef[:, :half], img_s, TN)
    g_oth[...] = dot(coef[:, half:], img_s, TN)


def mid_tile_kernel(width_t, *refs):
    imgs, old, new, refs = refs[:6], refs[6:8], refs[8:10], refs[10:]
    p_img, p_txt, p_oth, p_loss, g_img, g_txt, g_oth, loss_ref = refs
    cols_t, cols_s = slice(0, width_t), slice(width_t, None)
    img_s, add_s = stack(imgs, cols_s), stack(imgs[3:], cols_s)
    old_s, new_s = stack(old, cols_s), stack(new, cols_s)
    coef_i, loss_i = tile_terms(dot(stack(imgs, cols_t), stack(new, cols_t), NT), dot(img_s, new_s, NT))
    coef_t, loss_t = tile_terms(dot(stack(old, cols_t), stack(imgs[3:], cols_t), NT), dot(old_s, add_s, NT))
    loss_ref[...] = p_loss[...] + loss_i + loss_t
    some, half, add = p_img.shape[0], p_txt.shape[0], new[0].shape[0]
    grad = dot(coef_i, new_s)
    g_img[:some, :] = p_img[...] + grad[:some]
    g_img[some:, :] = grad[some:] + dot(coef_t, old_s, TN)
    for n, (part, ref) in enumerate(((p_txt, g_txt), (p_oth, g_oth))):
        ref[:half, :] = part[...] + dot(coef_t[n * half:(n + 1) * half], add_s)
        ref[half:, :] = dot(coef_i[:, n * add:(n + 1) * add], img_s, TN)


def last_coef_kernel(width_t, *refs):
    imgs, texts, last, (p_loss, coef_p, coef_t, loss_ref) = refs[:8], refs[8:12], refs[12], refs[13:]
    cols_t, cols_s = slice(0, width_t), slice(width_t, None)
    late = imgs[6:]
    part, loss_p = tile_terms(
        dot(stack(texts, cols_t), stack(late, cols_t), NT), dot(stack(texts, cols_s), stack(late, cols_s), NT)
    )
    coef_p[...] = part
    part, loss_t = tile_terms(
        dot(stack(imgs, cols_t), last[:, cols_t], NT), dot(stack(imgs, cols_s), last[:, cols_s], NT)
    )
    coef_t[...] = part
    loss_ref[...] = p_loss[...] + loss_p + loss_t


def end_coef_kernel(width_t, *refs):
    imgs, (last, p_loss, coef_u, loss_ref) = refs[:8], refs[8:]
    cols_t, cols_s = slice(0, width_t), slice(width_t, None)
    part, loss = tile_terms(
        dot(stack(imgs, cols_t), last[:, cols_t], NT), dot(stack(imgs, cols_s), last[:, cols_s], NT)
    )
    coef_u[...] = part
    loss_ref[...] = p_loss[...] + loss


def text_grad_kernel(width_t, core, *refs):
    imgs, (coef_p, coef_l, part, out) = refs[:8], refs[8:]
    cols_s = slice(width_t, None)
    most = part.shape[0]
    grad = part[...] + dot(coef_p[core * most:(core + 1) * most, :], stack(imgs[6:], cols_s))
    out[:most, :] = grad.astype(out.dtype)
    out[most:, :] = dot(coef_l[...], stack(imgs, cols_s), TN).astype(out.dtype)


def text_sum_kernel(own, from_core, t0, t1, t2, t3, t4):
    at = lambda low, high: own[low:high, :] + from_core[low:high, :].astype(f32)
    t0[...] = at(0, 256)
    t1[0:128, :] = at(256, 384).astype(bf16)
    t1[128:256, :] = at(640, 768).astype(bf16)
    t2[0:128, :] = at(384, 512).astype(bf16)
    t2[128:256, :] = at(768, 896).astype(bf16)
    t3[...] = at(512, 640)
    t4[...] = at(896, 1024).astype(bf16)


def image_grad_kernel(width_t, *refs):
    texts, last_t, last_u = refs[:4], refs[4], refs[5]
    coef_p, coef_t, coef_u, part, loss, i0, i1, i2, i3, i4 = refs[6:]
    cols_s = slice(width_t, None)
    most = part.shape[0]
    grad = dot(coef_t[...], last_t[:, cols_s]) + dot(coef_u[...], last_u[:, cols_s])
    early = part[...] + grad[:most]
    late = grad[most:] + dot(coef_p[...], stack(texts, cols_s), TN)
    i0[...] = early[0:256]
    i1[0:128, :] = early[256:384].astype(bf16)
    i1[128:256, :] = early[512:640].astype(bf16)
    i2[0:128, :] = early[640:768].astype(bf16)
    i2[128:256, :] = late[0:128].astype(bf16)
    i3[...] = early[384:512]
    i4[...] = late[128:256].astype(bf16)
    for ref in (i1, i2):
        put_pieces(ref, 256, loss[...])


def join(*parts):
    return jnp.concatenate(parts, axis=0)


def put_pieces(ref, row, value):
    ref[row:row + 16, :] = jnp.zeros((16, ref.shape[1]), bf16)
    first = value.astype(bf16)
    second = (value - first.astype(f32)).astype(bf16)
    third = (value - first.astype(f32) - second.astype(f32)).astype(bf16)
    ref[row:row + 16, 0:128] = jnp.concatenate([first, first], axis=0)
    ref[row:row + 16, 128:256] = jnp.concatenate([second, second], axis=0)
    ref[row:row + 16, 256:384] = jnp.concatenate([third, third], axis=0)


def get_pieces(ref, row):
    at = lambda k: ref[row:row + 16, k:k + 128].astype(f32)[:8]
    return at(0) + at(128) + at(256)


def image_sum_kernel(own, one, two, far, from_z, loss, loss_x, near, to_z, to_far, loss_out):
    rows = near.shape[0]
    loss_out[...] = loss[...] + loss_x[...] + get_pieces(one, 2 * rows) + get_pieces(two, 2 * rows)
    ring_sum(own, one, two, far, from_z, loss_out, near, to_z, to_far)


def ring_sum(own, one, two, far, from_z, loss, near, to_z, to_far):
    rows = near.shape[0]
    total = own[...] + one[:2 * rows, :].astype(f32) + two[:2 * rows, :].astype(f32)
    near[...] = total[:rows]
    to_z[:rows, :] = total[rows:].astype(bf16)
    put_pieces(to_z, rows, loss[...])
    to_far[...] = (far[...] + from_z[...].astype(f32)).astype(bf16)


def finish_kernel(
    scale_loss, loss, loss_far, txt, txt_z, txt_x, img, img_z, img_x, si, st, img_out, txt_out, loss_out
):
    rows = txt.shape[0]
    for stud, near, far, ring, out in ((si, img, img_z, img_x, img_out), (st, txt, txt_z, txt_x, txt_out)):
        wide = stud[...].astype(f32)
        norm = norm_of(wide)
        unit = wide / norm
        grad = near[...] + far[:rows, :].astype(f32) + ring[...].astype(f32)
        out[...] = (grad - jnp.sum(grad * unit, axis=-1, keepdims=True) * unit) / norm
    total = (loss[...] + loss_far[...]) + (get_pieces(img_z, rows) + get_pieces(txt_z, rows))
    loss_out[...] = jnp.sum(total, keepdims=True) * scale_loss + jnp.log(2.0)


def body(teacher_image, teacher_text, student_image, student_text):
    rows, width_t = teacher_image.shape
    width_s = student_image.shape[1]
    width = width_t + width_s
    img, txt = call(
        units_kernel, "units", (teacher_image, student_image, teacher_text, student_text),
        [((rows, width), bf16)] * 2,
        far=(teacher_image, student_image, teacher_text, student_text),
    )

    hold = lax.optimization_barrier
    run = functools.partial
    txt_l, img_l, txt_z, img_z = to_y(txt, 1), to_x(img, 1), to_text_z(txt), to_image_z(img)
    txt_r = to_y(txt, -1)
    txt_o, img_o = to_y(txt_l, 1), to_x(img_l, 1)
    txt_zl, img_zl = to_text_z(hold((txt_l, txt_z))[0]), to_image_z(hold((img_l, img_z))[0])
    img_r = to_x(hold((img, img_z))[0], -1)
    txt_zo, img_zo = to_text_z(txt_o), to_image_z(img_o)
    txt_zr, img_zr = to_y(hold((txt_z, txt_zl))[0], -1), to_x(hold((img_z, img_zl))[0], -1)
    txt_o, img_o, txt_zl, img_zl, img_r, txt_z, txt_l, txt_r = hold((txt_o, img_o, txt_zl, img_zl, img_r, txt_z, txt_l, txt_r))
    txt_1 = join(txt, txt_z, txt_l, txt_r)
    oth_1 = to_core(txt_1)
    pair_work = 2 * (width + 2 * width_s)
    grads = lambda *sizes: [((size * rows, width_s), f32) for size in sizes] + [((8, 128), f32)]
    imgs = [img, img_z, img_l]
    p_img, p_txt, p_oth, p_loss = call(
        run(near_tile_kernel, width_t), "near_tile", (*imgs, txt_1, oth_1), grads(3, 4, 4),
        flops=24 * rows * rows * pair_work,
    )
    txt_2 = join(txt_o, txt_zl)
    oth_2 = to_core(txt_2)
    imgs += [img_o, img_zl, img_r]
    p_img, p_txt, p_oth, p_loss = call(
        run(mid_tile_kernel, width_t), "mid_tile", (*imgs, txt_1, oth_1, txt_2, oth_2, p_img, p_txt, p_oth, p_loss),
        grads(6, 6, 6), limit=20, flops=48 * rows * rows * pair_work,
    )
    txt_zr, txt_zo, img_zo, img_zr, p_loss = hold((txt_zr, txt_zo, img_zo, img_zr, p_loss))
    txt_n = join(txt_zr, txt_zo)
    oth_n = to_core(txt_n)
    imgs += [img_zr, img_zo]
    texts = [txt_1, txt_2, oth_1, oth_2]
    coef_p, coef_t, loss = call(
        run(last_coef_kernel, width_t), "last_coef", (*imgs, *texts, txt_n, p_loss),
        [((12 * rows, 2 * rows), bf16), ((8 * rows, 2 * rows), bf16), ((8, 128), f32)], limit=24,
        flops=2 * (24 + 16) * rows * rows * width,
    )
    coef_u, loss = call(
        run(end_coef_kernel, width_t), "end_coef", (*imgs, oth_n, loss),
        [((8 * rows, 2 * rows), bf16), ((8, 128), f32)], flops=2 * 16 * rows * rows * width,
    )
    loss_core = to_core(loss)
    grad_work = 2 * (12 + 16) * rows * rows * width_s
    grad_o = call(
        run(text_grad_kernel, width_t, 1), "other_grad", (*imgs, coef_p, coef_u, p_oth),
        [((8 * rows, width_s), bf16)], flops=grad_work,
    )[0]
    grad_o, loss_core = hold((grad_o, loss_core))
    from_core = to_core(grad_o)
    loss = loss + loss_core
    loss = loss + to_y(loss, 1) + to_y(loss, -1) + to_y(loss, 2)
    pair = 2 * rows
    sums = [((rows, width_s), f32), ((rows, width_s), bf16)]
    grad_t = call(
        run(text_grad_kernel, width_t, 0), "text_grad", (*imgs, coef_p, coef_t, p_txt),
        [((8 * rows, width_s), f32)], flops=grad_work,
    )[0]
    t0, t1, t2, t3, t4 = call(
        text_sum_kernel, "text_sum", (grad_t, from_core),
        [((pair, width_s), f32)] + [((pair, width_s), bf16)] * 2 + sums,
    )
    i0, i1, i2, i3, i4 = call(
        run(image_grad_kernel, width_t), "image_grad", (*texts, txt_n, oth_n, coef_p, coef_t, coef_u, p_img, loss),
        [((pair, width_s), f32)] + [((pair + 16, width_s), bf16)] * 2 + sums, flops=2 * grad_work,
    )
    loss_x = to_x(loss, 2)
    i4, i1, i2 = to_image_z(i4), to_x(i1, -1), to_x(i2, 1)
    t1, t2, t4 = to_y(t1, -1), to_y(t2, 1), to_text_z(t4)
    parts = [((rows, width_s), f32), ((rows + 16, width_s), bf16), ((rows, width_s), bf16)]
    img, img_z, img_x, loss = call(
        image_sum_kernel, "image_sum", (i0, i1, i2, i3, i4, loss, loss_x), parts + [((8, 128), f32)],
    )
    txt, txt_z, txt_x = call(ring_sum, "text_ring_sum", (t0, t1, t2, t3, t4, loss), parts)
    txt_x, img_x = to_y(txt_x, 2), to_x(img_x, 2)
    txt_z, img_z, loss_far = to_text_z(txt_z), to_image_z(img_z), to_far_z(loss)
    pairs = float(rows * lax.axis_size("dp") * lax.axis_size("blk"))
    image_grad, text_grad, loss = call(
        functools.partial(finish_kernel, 1.0 / (pairs * pairs)), "finish",
        (loss, loss_far, txt, txt_z, txt_x, img, img_z, img_x, student_image, student_text),
        [((rows, width_s), f32)] * 2 + [((1, 1), f32)],
        keep=False,
    )
    return (image_grad, text_grad, loss.reshape(()))


def solution(mesh):
    spec = P(AXES, None)
    return jax.shard_map(body, mesh=mesh, in_specs=(spec,) * 4, out_specs=(spec, spec, P()), check_vma=False)
```

```python
import functools
import itertools

import jax
import jax.numpy as jnp
from jax import lax
from jax.experimental import pallas as pl
from jax.experimental.pallas import tpu as pltpu
from jax.sharding import PartitionSpec as P

eps = 1e-06
scale = 10.0
bias = -2.0
AXES = ("dp", "blk")
f32, bf16 = jnp.float32, jnp.bfloat16

ZH, Y, C, X, ZL = 2, 4, 2, 4, 2
NT = (((1,), (1,)), ((), ()))
TN = (((0,), (0,)), ((), ()))


def place(zh, y, c, x, zl):
    return ((zh * Y + y) * C + c) * (X * ZL) + x * ZL + zl


def permute(value, move):
    pairs = [
        (place(*at), place(*move(*at)))
        for at in itertools.product(range(ZH), range(Y), range(C), range(X), range(ZL))
    ]
    return lax.ppermute(value, AXES, pairs)


def to_x(value, step):
    return permute(value, lambda zh, y, c, x, zl: (zh, y, c, (x + step) % X, zl))


def to_y(value, step):
    return permute(value, lambda zh, y, c, x, zl: (zh, (y + step) % Y, c, x, zl))


def flip_x(value, bits):
    return permute(value, lambda zh, y, c, x, zl: (zh, y, c, x ^ bits, zl))


def flip_y(value, bits):
    return permute(value, lambda zh, y, c, x, zl: (zh, y ^ bits, c, x, zl))


def to_core(value):
    return permute(value, lambda zh, y, c, x, zl: (zh, y, 1 - c, x, zl))


def to_image_z(value):
    return permute(value, lambda zh, y, c, x, zl: (zh, y, c, x, 1 - zl))


def to_text_z(value):
    return permute(value, lambda zh, y, c, x, zl: (1 - zh, y, c, x, 1 - zl))


def to_far_z(value):
    return permute(value, lambda zh, y, c, x, zl: (1 - zh, y, c, x, zl))


def call(kernel, name, args, outs, limit=16, far=(), keep=True, flops=0, scratch=()):
    vmem = pl.BlockSpec(memory_space=pltpu.VMEM)
    near = [
        pltpu.with_memory_space_constraint(v, pltpu.HBM if any(v is w for w in far) else pltpu.VMEM) for v in args
    ]
    shape_of = pltpu.VMEM if keep else jax.ShapeDtypeStruct
    return pl.pallas_call(
        kernel,
        out_shape=tuple(shape_of(shape, dtype) for shape, dtype in outs),
        in_specs=[vmem] * len(args),
        out_specs=(vmem,) * len(outs),
        scratch_shapes=[pltpu.VMEM(shape, dtype) for shape, dtype in scratch],
        compiler_params=pltpu.CompilerParams(vmem_limit_bytes=limit * 2**20),
        cost_estimate=pl.CostEstimate(
            flops=flops, transcendentals=0, bytes_accessed=sum(v.size * v.dtype.itemsize for v in args),
        ),
        name=name,
    )(*near)


def norm_of(wide):
    return jnp.sqrt(jnp.sum(wide * wide, axis=-1, keepdims=True) + eps)


def units_kernel(ti, si, tt, st, img, txt):
    for teach, stud, out in ((ti, si, img), (tt, st, txt)):
        wide = teach[...].astype(f32)
        split = wide.shape[1]
        out[:, :split] = (wide / norm_of(wide)).astype(bf16)
        wide = stud[...].astype(f32)
        out[:, split:] = (wide / norm_of(wide)).astype(bf16)


def tile_terms(cos_t, cos_s):
    half_s = cos_s * (0.5 * scale) + 0.5 * bias
    tanh_t = jnp.tanh(cos_t * (0.5 * scale) + 0.5 * bias)
    tanh_s = jnp.tanh(half_s)
    coef = ((tanh_s - tanh_t) * (0.5 * scale)).astype(bf16)
    left = 1.0 - tanh_s
    for _ in range(3):
        rows = left.shape[0] // 2
        left = left[:rows] * left[rows:]
    line = half_s + half_s * tanh_t
    fold = lambda v: jnp.sum(v.reshape(-1, 8, v.shape[1]), axis=0)
    loss = -(fold(jnp.log(left)) + fold(line))
    return coef, sum(loss[:, k:k + 128] for k in range(0, loss.shape[1], 128))


def stack(refs, cols):
    return jnp.concatenate([r[:, cols] for r in refs], axis=0)


def dot(a, b, dims=(((1,), (0,)), ((), ()))):
    return lax.dot_general(a, b, dims, preferred_element_type=f32)


def near_tile_kernel(width_t, *refs):
    imgs, texts, (g_img, g_txt, g_oth, loss_ref) = refs[:3], refs[3:5], refs[5:]
    cols_t, cols_s = slice(0, width_t), slice(width_t, None)
    img_t, img_s, text_s = stack(imgs, cols_t), stack(imgs, cols_s), stack(texts, cols_s)
    coef, loss = tile_terms(dot(img_t, stack(texts, cols_t), NT), dot(img_s, text_s, NT))
    loss_ref[...] = loss
    g_img[...] = dot(coef, text_s)
    half = g_txt.shape[0]
    g_txt[...] = dot(coef[:, :half], img_s, TN)
    g_oth[...] = dot(coef[:, half:], img_s, TN)


def mid_tile_kernel(width_t, *refs):
    imgs, old, new, refs = refs[:6], refs[6:8], refs[8:10], refs[10:]
    p_img, p_txt, p_oth, p_loss, g_img, g_txt, g_oth, loss_ref = refs
    cols_t, cols_s = slice(0, width_t), slice(width_t, None)
    img_s, add_s = stack(imgs, cols_s), stack(imgs[3:], cols_s)
    old_s, new_s = stack(old, cols_s), stack(new, cols_s)
    coef_i, loss_i = tile_terms(dot(stack(imgs, cols_t), stack(new, cols_t), NT), dot(img_s, new_s, NT))
    coef_t, loss_t = tile_terms(dot(stack(old, cols_t), stack(imgs[3:], cols_t), NT), dot(old_s, add_s, NT))
    loss_ref[...] = p_loss[...] + loss_i + loss_t
    some, half, add = p_img.shape[0], p_txt.shape[0], new[0].shape[0]
    grad = dot(coef_i, new_s)
    g_img[:some, :] = p_img[...] + grad[:some]
    g_img[some:, :] = grad[some:] + dot(coef_t, old_s, TN)
    for n, (part, ref) in enumerate(((p_txt, g_txt), (p_oth, g_oth))):
        ref[:half, :] = part[...] + dot(coef_t[n * half:(n + 1) * half], add_s)
        ref[half:, :] = dot(coef_i[:, n * add:(n + 1) * add], img_s, TN)


def last_coef_kernel(width_t, *refs):
    imgs, texts, last, (p_loss, coef_p, coef_t, loss_ref) = refs[:8], refs[8:12], refs[12], refs[13:]
    cols_t, cols_s = slice(0, width_t), slice(width_t, None)
    late = imgs[6:]
    part, loss_p = tile_terms(
        dot(stack(texts, cols_t), stack(late, cols_t), NT), dot(stack(texts, cols_s), stack(late, cols_s), NT)
    )
    coef_p[...] = part
    part, loss_t = tile_terms(
        dot(stack(imgs, cols_t), last[:, cols_t], NT), dot(stack(imgs, cols_s), last[:, cols_s], NT)
    )
    coef_t[...] = part
    loss_ref[...] = p_loss[...] + loss_p + loss_t


def end_coef_kernel(width_t, *refs):
    imgs, (last, p_loss, coef_u, loss_ref) = refs[:8], refs[8:]
    cols_t, cols_s = slice(0, width_t), slice(width_t, None)
    part, loss = tile_terms(
        dot(stack(imgs, cols_t), last[:, cols_t], NT), dot(stack(imgs, cols_s), last[:, cols_s], NT)
    )
    coef_u[...] = part
    loss_ref[...] = p_loss[...] + loss


def text_grad_kernel(width_t, core, *refs):
    imgs, (coef_p, coef_l, part, out) = refs[:8], refs[8:]
    cols_s = slice(width_t, None)
    most = part.shape[0]
    grad = part[...] + dot(coef_p[core * most:(core + 1) * most, :], stack(imgs[6:], cols_s))
    out[:most, :] = grad.astype(out.dtype)
    out[most:, :] = dot(coef_l[...], stack(imgs, cols_s), TN).astype(out.dtype)


def text_sum_kernel(own, from_core, loss, t0, t1, t2, t3, t4):
    at = lambda low, high: own[low:high, :] + from_core[low:high, :].astype(f32)
    t0[...] = at(0, 256)
    t1[0:128, :] = at(256, 384).astype(bf16)
    t1[128:256, :] = at(640, 768).astype(bf16)
    t2[0:128, :] = at(384, 512).astype(bf16)
    t2[128:256, :] = at(768, 896).astype(bf16)
    t3[...] = at(512, 640)
    t4[...] = at(896, 1024).astype(bf16)
    for ref in (t1, t2):
        put_pieces(ref, 256, loss[...])


def image_grad_kernel(width_t, *refs):
    texts, last_t, last_u = refs[:4], refs[4], refs[5]
    coef_p, coef_t, coef_u, part, i0, i1, i2, i3, i4 = refs[6:]
    cols_s = slice(width_t, None)
    most = part.shape[0]
    grad = dot(coef_t[...], last_t[:, cols_s]) + dot(coef_u[...], last_u[:, cols_s])
    early = part[...] + grad[:most]
    late = grad[most:] + dot(coef_p[...], stack(texts, cols_s), TN)
    i0[...] = early[0:256]
    i1[0:128, :] = early[256:384].astype(bf16)
    i1[128:256, :] = early[512:640].astype(bf16)
    i2[0:128, :] = early[640:768].astype(bf16)
    i2[128:256, :] = late[0:128].astype(bf16)
    i3[...] = early[384:512]
    i4[...] = late[128:256].astype(bf16)


def join(*parts):
    return jnp.concatenate(parts, axis=0)


def put_pieces(ref, row, value):
    ref[row:row + 16, :] = jnp.zeros((16, ref.shape[1]), bf16)
    first = value.astype(bf16)
    second = (value - first.astype(f32)).astype(bf16)
    third = (value - first.astype(f32) - second.astype(f32)).astype(bf16)
    ref[row:row + 16, 0:128] = jnp.concatenate([first, first], axis=0)
    ref[row:row + 16, 128:256] = jnp.concatenate([second, second], axis=0)
    ref[row:row + 16, 256:384] = jnp.concatenate([third, third], axis=0)


def get_pieces(ref, row):
    at = lambda k: ref[row:row + 16, k:k + 128].astype(f32)[:8]
    return at(0) + at(128) + at(256)


def ring_sum(own, one, two, far, from_z, near, to_z, to_far):
    rows = near.shape[0]
    total = own[...] + one[:2 * rows, :].astype(f32) + two[:2 * rows, :].astype(f32)
    near[...] = total[:rows]
    to_z[:rows, :] = total[rows:].astype(bf16)
    to_far[...] = (far[...] + from_z[...].astype(f32)).astype(bf16)


def text_ring_kernel(own, one, two, far, from_z, loss, loss_far, img_z, near, to_z, to_far, img_out, loss_out):
    rows = near.shape[0]
    loss_out[...] = loss[...] + loss_far[...] + get_pieces(one, 2 * rows) + get_pieces(two, 2 * rows)
    ring_sum(own, one, two, far, from_z, near, to_z, to_far)
    img_out[:rows, :] = img_z[...]
    for ref in (to_z, img_out):
        put_pieces(ref, rows, loss_out[...])


def finish_kernel(
    scale_loss, loss, loss_far, txt, txt_z, txt_x, img, img_z, img_x, si, st, img_out, txt_out, loss_out
):
    rows = txt.shape[0]
    for stud, near, far, ring, out in ((si, img, img_z, img_x, img_out), (st, txt, txt_z, txt_x, txt_out)):
        wide = stud[...].astype(f32)
        norm = norm_of(wide)
        unit = wide / norm
        grad = near[...] + far[:rows, :].astype(f32) + ring[...].astype(f32)
        out[...] = (grad - jnp.sum(grad * unit, axis=-1, keepdims=True) * unit) / norm
    total = (loss[...] + loss_far[...]) + (get_pieces(img_z, rows) + get_pieces(txt_z, rows))
    loss_out[...] = jnp.sum(total, keepdims=True) * scale_loss + jnp.log(2.0)


def body(teacher_image, teacher_text, student_image, student_text):
    rows, width_t = teacher_image.shape
    width_s = student_image.shape[1]
    width = width_t + width_s
    img, txt = call(
        units_kernel, "units", (teacher_image, student_image, teacher_text, student_text),
        [((rows, width), bf16)] * 2,
        far=(teacher_image, student_image, teacher_text, student_text),
    )

    hold = lax.optimization_barrier
    run = functools.partial
    txt_l, img_l, txt_z, img_z = to_y(txt, 1), to_x(img, 1), to_text_z(txt), to_image_z(img)
    txt_r = to_y(txt, -1)
    txt_o, img_o = to_y(txt_l, 1), to_x(img_l, 1)
    txt_zl, img_zl = to_text_z(hold((txt_l, txt_z))[0]), to_image_z(hold((img_l, img_z))[0])
    img_r = to_x(hold((img, img_z))[0], -1)
    txt_zo, img_zo = to_text_z(txt_o), to_image_z(img_o)
    txt_zr, img_zr = to_y(hold((txt_z, txt_zl))[0], -1), to_x(hold((img_z, img_zl))[0], -1)
    txt_o, img_o, txt_zl, img_zl, img_r, txt_z, txt_l, txt_r = hold((txt_o, img_o, txt_zl, img_zl, img_r, txt_z, txt_l, txt_r))
    txt_1 = join(txt, txt_z, txt_l, txt_r)
    oth_1 = to_core(txt_1)
    pair_work = 2 * (width + 2 * width_s)
    grads = lambda *sizes: [((size * rows, width_s), f32) for size in sizes] + [((8, 128), f32)]
    imgs = [img, img_z, img_l]
    p_img, p_txt, p_oth, p_loss = call(
        run(near_tile_kernel, width_t), "near_tile", (*imgs, txt_1, oth_1), grads(3, 4, 4),
        flops=24 * rows * rows * pair_work,
    )
    txt_2 = join(txt_o, txt_zl)
    oth_2 = to_core(txt_2)
    imgs += [img_o, img_zl, img_r]
    p_img, p_txt, p_oth, p_loss = call(
        run(mid_tile_kernel, width_t), "mid_tile", (*imgs, txt_1, oth_1, txt_2, oth_2, p_img, p_txt, p_oth, p_loss),
        grads(6, 6, 6), limit=20, flops=48 * rows * rows * pair_work,
    )
    txt_zr, txt_zo, img_zo, img_zr, p_loss = hold((txt_zr, txt_zo, img_zo, img_zr, p_loss))
    txt_n = join(txt_zr, txt_zo)
    oth_n = to_core(txt_n)
    imgs += [img_zr, img_zo]
    texts = [txt_1, txt_2, oth_1, oth_2]
    coef_p, coef_t, loss = call(
        run(last_coef_kernel, width_t), "last_coef", (*imgs, *texts, txt_n, p_loss),
        [((12 * rows, 2 * rows), bf16), ((8 * rows, 2 * rows), bf16), ((8, 128), f32)], limit=24,
        flops=2 * (24 + 16) * rows * rows * width,
    )
    coef_u, loss = call(
        run(end_coef_kernel, width_t), "end_coef", (*imgs, oth_n, loss),
        [((8 * rows, 2 * rows), bf16), ((8, 128), f32)], flops=2 * 16 * rows * rows * width,
    )
    loss_core = to_core(loss)
    grad_work = 2 * (12 + 16) * rows * rows * width_s
    grad_o = call(
        run(text_grad_kernel, width_t, 1), "other_grad", (*imgs, coef_p, coef_u, p_oth),
        [((8 * rows, width_s), bf16)], flops=grad_work,
    )[0]
    grad_o, loss_core = hold((grad_o, loss_core))
    from_core = to_core(grad_o)
    loss = loss + loss_core
    loss_x = [to_x(loss, 1), to_x(loss, -1), to_x(loss, 2)]
    pair = 2 * rows
    sums = [((rows, width_s), f32), ((rows, width_s), bf16)]
    grad_t = call(
        run(text_grad_kernel, width_t, 0), "text_grad", (*imgs, coef_p, coef_t, p_txt),
        [((8 * rows, width_s), f32)], flops=grad_work,
    )[0]
    i0, i1, i2, i3, i4 = call(
        run(image_grad_kernel, width_t), "image_grad", (*texts, txt_n, oth_n, coef_p, coef_t, coef_u, p_img),
        [((pair, width_s), f32)] + [((pair, width_s), bf16)] * 2 + sums, flops=2 * grad_work,
    )
    loss_x, i0 = hold((loss_x, i0))
    loss = loss + loss_x[0] + loss_x[1] + loss_x[2]
    t0, t1, t2, t3, t4 = call(
        text_sum_kernel, "text_sum", (grad_t, from_core, loss),
        [((pair, width_s), f32)] + [((pair + 16, width_s), bf16)] * 2 + sums,
    )
    i4, i1, i2 = to_image_z(i4), to_x(i1, -1), to_x(i2, 1)
    loss_2 = to_y(loss, 2)
    t1, t2, t4 = to_y(t1, -1), to_y(t2, 1), to_text_z(t4)
    near, to_z, to_far = ((rows, width_s), f32), ((rows + 16, width_s), bf16), ((rows, width_s), bf16)
    img, img_z, img_x = call(ring_sum, "image_ring", (i0, i1, i2, i3, i4), [near, to_far, to_far])
    txt, txt_z, txt_x, img_z, loss = call(
        text_ring_kernel, "text_ring", (t0, t1, t2, t3, t4, loss, loss_2, img_z),
        [near, to_z, to_far, to_z, ((8, 128), f32)],
    )
    txt_x, img_x = to_y(txt_x, 2), to_x(img_x, 2)
    txt_z, img_z, loss_far = to_text_z(txt_z), to_image_z(img_z), to_far_z(loss)
    pairs = float(rows * lax.axis_size("dp") * lax.axis_size("blk"))
    image_grad, text_grad, loss = call(
        functools.partial(finish_kernel, 1.0 / (pairs * pairs)), "finish",
        (loss, loss_far, txt, txt_z, txt_x, img, img_z, img_x, student_image, student_text),
        [((rows, width_s), f32)] * 2 + [((1, 1), f32)],
        keep=False,
    )
    return (image_grad, text_grad, loss.reshape(()))


def solution(mesh):
    spec = P(AXES, None)
    return jax.shard_map(body, mesh=mesh, in_specs=(spec,) * 4, out_specs=(spec, spec, P()), check_vma=False)
```

```python
import functools
import itertools

import jax
import jax.numpy as jnp
from jax import lax
from jax.experimental import pallas as pl
from jax.experimental.pallas import tpu as pltpu
from jax.sharding import PartitionSpec as P

eps = 1e-06
scale = 10.0
bias = -2.0
AXES = ("dp", "blk")
f32, bf16 = jnp.float32, jnp.bfloat16

ZH, Y, C, X, ZL = 2, 4, 2, 4, 2
NT = (((1,), (1,)), ((), ()))
TN = (((0,), (0,)), ((), ()))


def place(zh, y, c, x, zl):
    return ((zh * Y + y) * C + c) * (X * ZL) + x * ZL + zl


def permute(value, move):
    pairs = [
        (place(*at), place(*move(*at)))
        for at in itertools.product(range(ZH), range(Y), range(C), range(X), range(ZL))
    ]
    return lax.ppermute(value, AXES, pairs)


def to_x(value, step):
    return permute(value, lambda zh, y, c, x, zl: (zh, y, c, (x + step) % X, zl))


def to_y(value, step):
    return permute(value, lambda zh, y, c, x, zl: (zh, (y + step) % Y, c, x, zl))


def flip_x(value, bits):
    return permute(value, lambda zh, y, c, x, zl: (zh, y, c, x ^ bits, zl))


def flip_y(value, bits):
    return permute(value, lambda zh, y, c, x, zl: (zh, y ^ bits, c, x, zl))


def to_core(value):
    return permute(value, lambda zh, y, c, x, zl: (zh, y, 1 - c, x, zl))


def to_image_z(value):
    return permute(value, lambda zh, y, c, x, zl: (zh, y, c, x, 1 - zl))


def to_text_z(value):
    return permute(value, lambda zh, y, c, x, zl: (1 - zh, y, c, x, 1 - zl))


def to_far_z(value):
    return permute(value, lambda zh, y, c, x, zl: (1 - zh, y, c, x, zl))


def call(kernel, name, args, outs, limit=16, far=(), keep=True, flops=0, scratch=()):
    vmem = pl.BlockSpec(memory_space=pltpu.VMEM)
    near = [
        pltpu.with_memory_space_constraint(v, pltpu.HBM if any(v is w for w in far) else pltpu.VMEM) for v in args
    ]
    shape_of = pltpu.VMEM if keep else jax.ShapeDtypeStruct
    return pl.pallas_call(
        kernel,
        out_shape=tuple(shape_of(shape, dtype) for shape, dtype in outs),
        in_specs=[vmem] * len(args),
        out_specs=(vmem,) * len(outs),
        scratch_shapes=[pltpu.VMEM(shape, dtype) for shape, dtype in scratch],
        compiler_params=pltpu.CompilerParams(vmem_limit_bytes=limit * 2**20),
        cost_estimate=pl.CostEstimate(
            flops=flops, transcendentals=0, bytes_accessed=sum(v.size * v.dtype.itemsize for v in args),
        ),
        name=name,
    )(*near)


def norm_of(wide):
    return jnp.sqrt(jnp.sum(wide * wide, axis=-1, keepdims=True) + eps)


def units_kernel(ti, si, tt, st, img, txt):
    for teach, stud, out in ((ti, si, img), (tt, st, txt)):
        wide = teach[...].astype(f32)
        split = wide.shape[1]
        out[:, :split] = (wide / norm_of(wide)).astype(bf16)
        wide = stud[...].astype(f32)
        out[:, split:] = (wide / norm_of(wide)).astype(bf16)


def tile_terms(cos_t, cos_s):
    half_s = cos_s * (0.5 * scale) + 0.5 * bias
    tanh_t = jnp.tanh(cos_t * (0.5 * scale) + 0.5 * bias)
    tanh_s = jnp.tanh(half_s)
    coef = ((tanh_s - tanh_t) * (0.5 * scale)).astype(bf16)
    left = 1.0 - tanh_s
    for _ in range(3):
        rows = left.shape[0] // 2
        left = left[:rows] * left[rows:]
    line = half_s + half_s * tanh_t
    fold = lambda v: jnp.sum(v.reshape(-1, 8, v.shape[1]), axis=0)
    loss = -(fold(jnp.log(left)) + fold(line))
    return coef, sum(loss[:, k:k + 128] for k in range(0, loss.shape[1], 128))


def stack(refs, cols):
    return jnp.concatenate([r[:, cols] for r in refs], axis=0)


def dot(a, b, dims=(((1,), (0,)), ((), ()))):
    return lax.dot_general(a, b, dims, preferred_element_type=f32)


def near_tile_kernel(width_t, *refs):
    imgs, texts, (g_img, g_txt, g_oth, loss_ref) = refs[:3], refs[3:5], refs[5:]
    cols_t, cols_s = slice(0, width_t), slice(width_t, None)
    img_t, img_s, text_s = stack(imgs, cols_t), stack(imgs, cols_s), stack(texts, cols_s)
    coef, loss = tile_terms(dot(img_t, stack(texts, cols_t), NT), dot(img_s, text_s, NT))
    loss_ref[...] = loss
    g_img[...] = dot(coef, text_s)
    half = g_txt.shape[0]
    g_txt[...] = dot(coef[:, :half], img_s, TN)
    g_oth[...] = dot(coef[:, half:], img_s, TN)


def mid_tile_kernel(width_t, *refs):
    imgs, old, new, refs = refs[:6], refs[6:8], refs[8:10], refs[10:]
    p_img, p_txt, p_oth, p_loss, g_img, g_txt, g_oth, loss_ref = refs
    cols_t, cols_s = slice(0, width_t), slice(width_t, None)
    img_s, add_s = stack(imgs, cols_s), stack(imgs[3:], cols_s)
    old_s, new_s = stack(old, cols_s), stack(new, cols_s)
    coef_i, loss_i = tile_terms(dot(stack(imgs, cols_t), stack(new, cols_t), NT), dot(img_s, new_s, NT))
    coef_t, loss_t = tile_terms(dot(stack(old, cols_t), stack(imgs[3:], cols_t), NT), dot(old_s, add_s, NT))
    loss_ref[...] = p_loss[...] + loss_i + loss_t
    some, half, add = p_img.shape[0], p_txt.shape[0], new[0].shape[0]
    grad = dot(coef_i, new_s)
    g_img[:some, :] = p_img[...] + grad[:some]
    g_img[some:, :] = grad[some:] + dot(coef_t, old_s, TN)
    for n, (part, ref) in enumerate(((p_txt, g_txt), (p_oth, g_oth))):
        ref[:half, :] = part[...] + dot(coef_t[n * half:(n + 1) * half], add_s)
        ref[half:, :] = dot(coef_i[:, n * add:(n + 1) * add], img_s, TN)


def last_coef_kernel(width_t, *refs):
    imgs, texts, last, (p_loss, coef_p, coef_t, loss_ref) = refs[:8], refs[8:12], refs[12], refs[13:]
    cols_t, cols_s = slice(0, width_t), slice(width_t, None)
    late = imgs[6:]
    part, loss_p = tile_terms(
        dot(stack(texts, cols_t), stack(late, cols_t), NT), dot(stack(texts, cols_s), stack(late, cols_s), NT)
    )
    coef_p[...] = part
    part, loss_t = tile_terms(
        dot(stack(imgs, cols_t), last[:, cols_t], NT), dot(stack(imgs, cols_s), last[:, cols_s], NT)
    )
    coef_t[...] = part
    loss_ref[...] = p_loss[...] + loss_p + loss_t


def end_coef_kernel(width_t, *refs):
    imgs, (last, p_loss, coef_u, loss_ref) = refs[:8], refs[8:]
    cols_t, cols_s = slice(0, width_t), slice(width_t, None)
    part, loss = tile_terms(
        dot(stack(imgs, cols_t), last[:, cols_t], NT), dot(stack(imgs, cols_s), last[:, cols_s], NT)
    )
    coef_u[...] = part
    loss_ref[...] = p_loss[...] + loss


def text_grad_kernel(width_t, core, *refs):
    imgs, (coef_p, coef_l, part, out) = refs[:8], refs[8:]
    cols_s = slice(width_t, None)
    most = part.shape[0]
    grad = part[...] + dot(coef_p[core * most:(core + 1) * most, :], stack(imgs[6:], cols_s))
    out[:most, :] = grad.astype(out.dtype)
    out[most:, :] = dot(coef_l[...], stack(imgs, cols_s), TN).astype(out.dtype)


def text_sum_kernel(own, from_core, loss, t0, t1, t2, t3, t4):
    at = lambda low, high: own[low:high, :] + from_core[low:high, :]
    t0[...] = at(0, 256)
    t1[0:128, :] = at(256, 384).astype(bf16)
    t1[128:256, :] = at(640, 768).astype(bf16)
    t2[0:128, :] = at(384, 512).astype(bf16)
    t2[128:256, :] = at(768, 896).astype(bf16)
    t3[...] = at(512, 640)
    t4[...] = at(896, 1024).astype(bf16)
    for ref in (t1, t2):
        put_pieces(ref, 256, loss[...])


def image_grad_kernel(width_t, *refs):
    texts, last_t, last_u = refs[:4], refs[4], refs[5]
    coef_p, coef_t, coef_u, part, i0, i1, i2, i3, i4 = refs[6:]
    cols_s = slice(width_t, None)
    most = part.shape[0]
    grad = dot(coef_t[...], last_t[:, cols_s]) + dot(coef_u[...], last_u[:, cols_s])
    early = part[...] + grad[:most]
    late = grad[most:] + dot(coef_p[...], stack(texts, cols_s), TN)
    i0[...] = early[0:256]
    i1[0:128, :] = early[256:384].astype(bf16)
    i1[128:256, :] = early[512:640].astype(bf16)
    i2[0:128, :] = early[640:768].astype(bf16)
    i2[128:256, :] = late[0:128].astype(bf16)
    i3[...] = early[384:512]
    i4[...] = late[128:256].astype(bf16)


def join(*parts):
    return jnp.concatenate(parts, axis=0)


def put_pieces(ref, row, value):
    ref[row:row + 16, :] = jnp.zeros((16, ref.shape[1]), bf16)
    first = value.astype(bf16)
    second = (value - first.astype(f32)).astype(bf16)
    third = (value - first.astype(f32) - second.astype(f32)).astype(bf16)
    ref[row:row + 16, 0:128] = jnp.concatenate([first, first], axis=0)
    ref[row:row + 16, 128:256] = jnp.concatenate([second, second], axis=0)
    ref[row:row + 16, 256:384] = jnp.concatenate([third, third], axis=0)


def get_pieces(ref, row):
    at = lambda k: ref[row:row + 16, k:k + 128].astype(f32)[:8]
    return at(0) + at(128) + at(256)


def ring_sum(own, one, two, far, from_z, near, to_z, to_far):
    rows = near.shape[0]
    total = own[...] + one[:2 * rows, :].astype(f32) + two[:2 * rows, :].astype(f32)
    near[...] = total[:rows]
    to_z[:rows, :] = total[rows:].astype(bf16)
    to_far[...] = (far[...] + from_z[...].astype(f32)).astype(bf16)


def text_ring_kernel(own, one, two, far, from_z, loss, loss_far, img_z, near, to_z, to_far, img_out, loss_out):
    rows = near.shape[0]
    loss_out[...] = loss[...] + loss_far[...] + get_pieces(one, 2 * rows) + get_pieces(two, 2 * rows)
    ring_sum(own, one, two, far, from_z, near, to_z, to_far)
    img_out[:rows, :] = img_z[...]
    for ref in (to_z, img_out):
        put_pieces(ref, rows, loss_out[...])


def finish_kernel(
    scale_loss, loss, loss_far, txt, txt_z, txt_x, img, img_z, img_x, si, st, img_out, txt_out, loss_out
):
    rows = txt.shape[0]
    for stud, near, far, ring, out in ((si, img, img_z, img_x, img_out), (st, txt, txt_z, txt_x, txt_out)):
        wide = stud[...].astype(f32)
        norm = norm_of(wide)
        unit = wide / norm
        grad = near[...] + far[:rows, :].astype(f32) + ring[...].astype(f32)
        out[...] = (grad - jnp.sum(grad * unit, axis=-1, keepdims=True) * unit) / norm
    total = (loss[...] + loss_far[...]) + (get_pieces(img_z, rows) + get_pieces(txt_z, rows))
    loss_out[...] = jnp.sum(total, keepdims=True) * scale_loss + jnp.log(2.0)


def body(teacher_image, teacher_text, student_image, student_text):
    rows, width_t = teacher_image.shape
    width_s = student_image.shape[1]
    width = width_t + width_s
    img, txt = call(
        units_kernel, "units", (teacher_image, student_image, teacher_text, student_text),
        [((rows, width), bf16)] * 2,
        far=(teacher_image, student_image, teacher_text, student_text),
    )

    hold = lax.optimization_barrier
    run = functools.partial
    txt_l, img_l, txt_z, img_z = to_y(txt, 1), to_x(img, 1), to_text_z(txt), to_image_z(img)
    txt_r = to_y(txt, -1)
    txt_o, img_o = to_y(txt_l, 1), to_x(img_l, 1)
    txt_zl, img_zl = to_text_z(hold((txt_l, txt_z))[0]), to_image_z(hold((img_l, img_z))[0])
    img_r = to_x(hold((img, img_z))[0], -1)
    txt_zo, img_zo = to_text_z(txt_o), to_image_z(img_o)
    txt_zr, img_zr = to_y(hold((txt_z, txt_zl))[0], -1), to_x(hold((img_z, img_zl))[0], -1)
    txt_o, img_o, txt_zl, img_zl, img_r, txt_z, txt_l, txt_r = hold((txt_o, img_o, txt_zl, img_zl, img_r, txt_z, txt_l, txt_r))
    txt_1 = join(txt, txt_z, txt_l, txt_r)
    oth_1 = to_core(txt_1)
    pair_work = 2 * (width + 2 * width_s)
    grads = lambda *sizes: [((size * rows, width_s), f32) for size in sizes] + [((8, 128), f32)]
    imgs = [img, img_z, img_l]
    p_img, p_txt, p_oth, p_loss = call(
        run(near_tile_kernel, width_t), "near_tile", (*imgs, txt_1, oth_1), grads(3, 4, 4),
        flops=24 * rows * rows * pair_work,
    )
    txt_2 = join(txt_o, txt_zl)
    oth_2 = to_core(txt_2)
    imgs += [img_o, img_zl, img_r]
    p_img, p_txt, p_oth, p_loss = call(
        run(mid_tile_kernel, width_t), "mid_tile", (*imgs, txt_1, oth_1, txt_2, oth_2, p_img, p_txt, p_oth, p_loss),
        grads(6, 6, 6), limit=20, flops=48 * rows * rows * pair_work,
    )
    txt_zr, txt_zo, img_zo, img_zr, p_loss = hold((txt_zr, txt_zo, img_zo, img_zr, p_loss))
    txt_n = join(txt_zr, txt_zo)
    oth_n = to_core(txt_n)
    imgs += [img_zr, img_zo]
    texts = [txt_1, txt_2, oth_1, oth_2]
    coef_p, coef_t, loss = call(
        run(last_coef_kernel, width_t), "last_coef", (*imgs, *texts, txt_n, p_loss),
        [((12 * rows, 2 * rows), bf16), ((8 * rows, 2 * rows), bf16), ((8, 128), f32)], limit=24,
        flops=2 * (24 + 16) * rows * rows * width,
    )
    coef_u, loss = call(
        run(end_coef_kernel, width_t), "end_coef", (*imgs, oth_n, loss),
        [((8 * rows, 2 * rows), bf16), ((8, 128), f32)], flops=2 * 16 * rows * rows * width,
    )
    loss_core = to_core(loss)
    grad_work = 2 * (12 + 16) * rows * rows * width_s
    grad_o = call(
        run(text_grad_kernel, width_t, 1), "other_grad", (*imgs, coef_p, coef_u, p_oth),
        [((8 * rows, width_s), f32)], flops=grad_work,
    )[0]
    grad_o, loss_core = hold((grad_o, loss_core))
    from_core = to_core(grad_o)
    loss = loss + loss_core
    loss_x = [to_x(loss, 1), to_x(loss, -1), to_x(loss, 2)]
    pair = 2 * rows
    sums = [((rows, width_s), f32), ((rows, width_s), bf16)]
    grad_t = call(
        run(text_grad_kernel, width_t, 0), "text_grad", (*imgs, coef_p, coef_t, p_txt),
        [((8 * rows, width_s), f32)], flops=grad_work,
    )[0]
    i0, i1, i2, i3, i4 = call(
        run(image_grad_kernel, width_t), "image_grad", (*texts, txt_n, oth_n, coef_p, coef_t, coef_u, p_img),
        [((pair, width_s), f32)] + [((pair, width_s), bf16)] * 2 + sums, flops=2 * grad_work,
    )
    loss_x, i0 = hold((loss_x, i0))
    loss = loss + loss_x[0] + loss_x[1] + loss_x[2]
    t0, t1, t2, t3, t4 = call(
        text_sum_kernel, "text_sum", (grad_t, from_core, loss),
        [((pair, width_s), f32)] + [((pair + 16, width_s), bf16)] * 2 + sums,
    )
    i4, i1, i2 = to_image_z(i4), to_x(i1, -1), to_x(i2, 1)
    loss_2 = to_y(loss, 2)
    t1, t2, t4 = to_y(t1, -1), to_y(t2, 1), to_text_z(t4)
    near, to_z, to_far = ((rows, width_s), f32), ((rows + 16, width_s), bf16), ((rows, width_s), bf16)
    img, img_z, img_x = call(ring_sum, "image_ring", (i0, i1, i2, i3, i4), [near, to_far, to_far])
    txt, txt_z, txt_x, img_z, loss = call(
        text_ring_kernel, "text_ring", (t0, t1, t2, t3, t4, loss, loss_2, img_z),
        [near, to_z, to_far, to_z, ((8, 128), f32)],
    )
    txt_x, img_x = to_y(txt_x, 2), to_x(img_x, 2)
    txt_z, img_z, loss_far = to_text_z(txt_z), to_image_z(img_z), to_far_z(loss)
    pairs = float(rows * lax.axis_size("dp") * lax.axis_size("blk"))
    image_grad, text_grad, loss = call(
        functools.partial(finish_kernel, 1.0 / (pairs * pairs)), "finish",
        (loss, loss_far, txt, txt_z, txt_x, img, img_z, img_x, student_image, student_text),
        [((rows, width_s), f32)] * 2 + [((1, 1), f32)],
        keep=False,
    )
    return (image_grad, text_grad, loss.reshape(()))


def solution(mesh):
    spec = P(AXES, None)
    return jax.shard_map(body, mesh=mesh, in_specs=(spec,) * 4, out_specs=(spec, spec, P()), check_vma=False)
```

```python
import functools
import itertools

import jax
import jax.numpy as jnp
from jax import lax
from jax.experimental import pallas as pl
from jax.experimental.pallas import tpu as pltpu
from jax.sharding import PartitionSpec as P

eps = 1e-06
scale = 10.0
bias = -2.0
AXES = ("dp", "blk")
f32, bf16 = jnp.float32, jnp.bfloat16

ZH, Y, C, X, ZL = 2, 4, 2, 4, 2
NT = (((1,), (1,)), ((), ()))
TN = (((0,), (0,)), ((), ()))


def place(zh, y, c, x, zl):
    return ((zh * Y + y) * C + c) * (X * ZL) + x * ZL + zl


def permute(value, move):
    pairs = [
        (place(*at), place(*move(*at)))
        for at in itertools.product(range(ZH), range(Y), range(C), range(X), range(ZL))
    ]
    return lax.ppermute(value, AXES, pairs)


def to_x(value, step):
    return permute(value, lambda zh, y, c, x, zl: (zh, y, c, (x + step) % X, zl))


def to_y(value, step):
    return permute(value, lambda zh, y, c, x, zl: (zh, (y + step) % Y, c, x, zl))


def flip_x(value, bits):
    return permute(value, lambda zh, y, c, x, zl: (zh, y, c, x ^ bits, zl))


def flip_y(value, bits):
    return permute(value, lambda zh, y, c, x, zl: (zh, y ^ bits, c, x, zl))


def to_core(value):
    return permute(value, lambda zh, y, c, x, zl: (zh, y, 1 - c, x, zl))


def to_image_z(value):
    return permute(value, lambda zh, y, c, x, zl: (zh, y, c, x, 1 - zl))


def to_text_z(value):
    return permute(value, lambda zh, y, c, x, zl: (1 - zh, y, c, x, 1 - zl))


def to_far_z(value):
    return permute(value, lambda zh, y, c, x, zl: (1 - zh, y, c, x, zl))


def call(kernel, name, args, outs, limit=16, far=(), keep=True, flops=0, scratch=()):
    vmem = pl.BlockSpec(memory_space=pltpu.VMEM)
    near = [
        pltpu.with_memory_space_constraint(v, pltpu.HBM if any(v is w for w in far) else pltpu.VMEM) for v in args
    ]
    shape_of = pltpu.VMEM if keep else jax.ShapeDtypeStruct
    return pl.pallas_call(
        kernel,
        out_shape=tuple(shape_of(shape, dtype) for shape, dtype in outs),
        in_specs=[vmem] * len(args),
        out_specs=(vmem,) * len(outs),
        scratch_shapes=[pltpu.VMEM(shape, dtype) for shape, dtype in scratch],
        compiler_params=pltpu.CompilerParams(vmem_limit_bytes=limit * 2**20),
        cost_estimate=pl.CostEstimate(
            flops=flops, transcendentals=0, bytes_accessed=sum(v.size * v.dtype.itemsize for v in args),
        ),
        name=name,
    )(*near)


def norm_of(wide):
    return jnp.sqrt(jnp.sum(wide * wide, axis=-1, keepdims=True) + eps)


def units_kernel(ti, si, tt, st, img, txt):
    for teach, stud, out in ((ti, si, img), (tt, st, txt)):
        wide = teach[...].astype(f32)
        split = wide.shape[1]
        out[:, :split] = (wide / norm_of(wide)).astype(bf16)
        wide = stud[...].astype(f32)
        out[:, split:] = (wide / norm_of(wide)).astype(bf16)


def tile_terms(cos_t, cos_s):
    half_s = cos_s * (0.5 * scale) + 0.5 * bias
    tanh_t = jnp.tanh(cos_t * (0.5 * scale) + 0.5 * bias)
    tanh_s = jnp.tanh(half_s)
    coef = ((tanh_s - tanh_t) * (0.5 * scale)).astype(bf16)
    left = 1.0 - tanh_s
    for _ in range(3):
        rows = left.shape[0] // 2
        left = left[:rows] * left[rows:]
    line = half_s + half_s * tanh_t
    fold = lambda v: jnp.sum(v.reshape(-1, 8, v.shape[1]), axis=0)
    loss = -(fold(jnp.log(left)) + fold(line))
    return coef, sum(loss[:, k:k + 128] for k in range(0, loss.shape[1], 128))


def stack(refs, cols):
    return jnp.concatenate([r[:, cols] for r in refs], axis=0)


def dot(a, b, dims=(((1,), (0,)), ((), ()))):
    return lax.dot_general(a, b, dims, preferred_element_type=f32)


def near_tile_kernel(width_t, *refs):
    imgs, texts, (g_img, g_txt, g_oth, loss_ref) = refs[:3], refs[3:5], refs[5:]
    cols_t, cols_s = slice(0, width_t), slice(width_t, None)
    img_t, img_s, text_s = stack(imgs, cols_t), stack(imgs, cols_s), stack(texts, cols_s)
    coef, loss = tile_terms(dot(img_t, stack(texts, cols_t), NT), dot(img_s, text_s, NT))
    loss_ref[...] = loss
    g_img[...] = dot(coef, text_s)
    half = g_txt.shape[0]
    g_txt[...] = dot(coef[:, :half], img_s, TN)
    g_oth[...] = dot(coef[:, half:], img_s, TN)


def mid_tile_kernel(width_t, *refs):
    imgs, old, new, refs = refs[:6], refs[6:8], refs[8:10], refs[10:]
    p_img, p_txt, p_oth, p_loss, g_img, g_txt, g_oth, loss_ref = refs
    cols_t, cols_s = slice(0, width_t), slice(width_t, None)
    img_s, add_s = stack(imgs, cols_s), stack(imgs[3:], cols_s)
    old_s, new_s = stack(old, cols_s), stack(new, cols_s)
    coef_i, loss_i = tile_terms(dot(stack(imgs, cols_t), stack(new, cols_t), NT), dot(img_s, new_s, NT))
    coef_t, loss_t = tile_terms(dot(stack(old, cols_t), stack(imgs[3:], cols_t), NT), dot(old_s, add_s, NT))
    loss_ref[...] = p_loss[...] + loss_i + loss_t
    some, half, add = p_img.shape[0], p_txt.shape[0], new[0].shape[0]
    grad = dot(coef_i, new_s)
    g_img[:some, :] = p_img[...] + grad[:some]
    g_img[some:, :] = grad[some:] + dot(coef_t, old_s, TN)
    for n, (part, ref) in enumerate(((p_txt, g_txt), (p_oth, g_oth))):
        ref[:half, :] = part[...] + dot(coef_t[n * half:(n + 1) * half], add_s)
        ref[half:, :] = dot(coef_i[:, n * add:(n + 1) * add], img_s, TN)


def coef_blocks(width_t, rows, cols, out, size):
    cols_t, cols_s = slice(0, width_t), slice(width_t, None)
    right_t, right_s = stack(cols, cols_t), stack(cols, cols_s)
    left_t, left_s = stack(rows, cols_t), stack(rows, cols_s)
    total = jnp.zeros((8, 128), f32)
    for at in range(0, left_t.shape[0], size):
        part = slice(at, at + size)
        coef, loss = tile_terms(dot(left_t[part], right_t, NT), dot(left_s[part], right_s, NT))
        out[part, :] = coef
        total = total + loss
    return total


def last_coef_kernel(width_t, *refs):
    imgs, texts, last, (p_loss, coef_p, coef_t, loss_ref) = refs[:8], refs[8:12], refs[12], refs[13:]
    loss = coef_blocks(width_t, texts, imgs[6:], coef_p, 256) + coef_blocks(width_t, imgs, [last], coef_t, 256)
    loss_ref[...] = p_loss[...] + loss


def end_coef_kernel(width_t, *refs):
    imgs, (last, p_loss, coef_u, loss_ref) = refs[:8], refs[8:]
    loss_ref[...] = p_loss[...] + coef_blocks(width_t, imgs, [last], coef_u, 256)


def text_grad_kernel(width_t, core, *refs):
    imgs, (coef_p, coef_l, part, out) = refs[:8], refs[8:]
    cols_s = slice(width_t, None)
    most = part.shape[0]
    grad = part[...] + dot(coef_p[core * most:(core + 1) * most, :], stack(imgs[6:], cols_s))
    out[:most, :] = grad.astype(out.dtype)
    out[most:, :] = dot(coef_l[...], stack(imgs, cols_s), TN).astype(out.dtype)


def text_sum_kernel(own, from_core, loss, t0, t1, t2, t3, t4):
    at = lambda low, high: own[low:high, :] + from_core[low:high, :].astype(f32)
    t0[...] = at(0, 256)
    t1[0:128, :] = at(256, 384).astype(bf16)
    t1[128:256, :] = at(640, 768).astype(bf16)
    t2[0:128, :] = at(384, 512).astype(bf16)
    t2[128:256, :] = at(768, 896).astype(bf16)
    t3[...] = at(512, 640)
    t4[...] = at(896, 1024).astype(bf16)
    for ref in (t1, t2):
        put_pieces(ref, 256, loss[...])


def image_grad_kernel(width_t, *refs):
    texts, last_t, last_u = refs[:4], refs[4], refs[5]
    coef_p, coef_t, coef_u, part, i0, i1, i2, i3, i4 = refs[6:]
    cols_s = slice(width_t, None)
    most = part.shape[0]
    grad = dot(coef_t[...], last_t[:, cols_s]) + dot(coef_u[...], last_u[:, cols_s])
    early = part[...] + grad[:most]
    late = grad[most:] + dot(coef_p[...], stack(texts, cols_s), TN)
    i0[...] = early[0:256]
    i1[0:128, :] = early[256:384].astype(bf16)
    i1[128:256, :] = early[512:640].astype(bf16)
    i2[0:128, :] = early[640:768].astype(bf16)
    i2[128:256, :] = late[0:128].astype(bf16)
    i3[...] = early[384:512]
    i4[...] = late[128:256].astype(bf16)


def join(*parts):
    return jnp.concatenate(parts, axis=0)


def put_pieces(ref, row, value):
    ref[row:row + 16, :] = jnp.zeros((16, ref.shape[1]), bf16)
    first = value.astype(bf16)
    second = (value - first.astype(f32)).astype(bf16)
    third = (value - first.astype(f32) - second.astype(f32)).astype(bf16)
    ref[row:row + 16, 0:128] = jnp.concatenate([first, first], axis=0)
    ref[row:row + 16, 128:256] = jnp.concatenate([second, second], axis=0)
    ref[row:row + 16, 256:384] = jnp.concatenate([third, third], axis=0)


def get_pieces(ref, row):
    at = lambda k: ref[row:row + 16, k:k + 128].astype(f32)[:8]
    return at(0) + at(128) + at(256)


def ring_sum(own, one, two, far, from_z, near, to_z, to_far):
    rows = near.shape[0]
    total = own[...] + one[:2 * rows, :].astype(f32) + two[:2 * rows, :].astype(f32)
    near[...] = total[:rows]
    to_z[:rows, :] = total[rows:].astype(bf16)
    to_far[...] = (far[...] + from_z[...].astype(f32)).astype(bf16)


def text_ring_kernel(own, one, two, far, from_z, loss, loss_far, img_z, near, to_z, to_far, img_out, loss_out):
    rows = near.shape[0]
    loss_out[...] = loss[...] + loss_far[...] + get_pieces(one, 2 * rows) + get_pieces(two, 2 * rows)
    ring_sum(own, one, two, far, from_z, near, to_z, to_far)
    img_out[:rows, :] = img_z[...]
    for ref in (to_z, img_out):
        put_pieces(ref, rows, loss_out[...])


def finish_kernel(
    scale_loss, loss, loss_far, txt, txt_z, txt_x, img, img_z, img_x, si, st, img_out, txt_out, loss_out
):
    rows = txt.shape[0]
    for stud, near, far, ring, out in ((si, img, img_z, img_x, img_out), (st, txt, txt_z, txt_x, txt_out)):
        wide = stud[...].astype(f32)
        norm = norm_of(wide)
        unit = wide / norm
        grad = near[...] + far[:rows, :].astype(f32) + ring[...].astype(f32)
        out[...] = (grad - jnp.sum(grad * unit, axis=-1, keepdims=True) * unit) / norm
    total = (loss[...] + loss_far[...]) + (get_pieces(img_z, rows) + get_pieces(txt_z, rows))
    loss_out[...] = jnp.sum(total, keepdims=True) * scale_loss + jnp.log(2.0)


def body(teacher_image, teacher_text, student_image, student_text):
    rows, width_t = teacher_image.shape
    width_s = student_image.shape[1]
    width = width_t + width_s
    img, txt = call(
        units_kernel, "units", (teacher_image, student_image, teacher_text, student_text),
        [((rows, width), bf16)] * 2,
        far=(teacher_image, student_image, teacher_text, student_text),
    )

    hold = lax.optimization_barrier
    run = functools.partial
    txt_l, img_l, txt_z, img_z = to_y(txt, 1), to_x(img, 1), to_text_z(txt), to_image_z(img)
    txt_r = to_y(txt, -1)
    txt_o, img_o = to_y(txt_l, 1), to_x(img_l, 1)
    txt_zl, img_zl = to_text_z(hold((txt_l, txt_z))[0]), to_image_z(hold((img_l, img_z))[0])
    img_r = to_x(hold((img, img_z))[0], -1)
    txt_zo, img_zo = to_text_z(txt_o), to_image_z(img_o)
    txt_zr, img_zr = to_y(hold((txt_z, txt_zl))[0], -1), to_x(hold((img_z, img_zl))[0], -1)
    txt_o, img_o, txt_zl, img_zl, img_r, txt_z, txt_l, txt_r = hold((txt_o, img_o, txt_zl, img_zl, img_r, txt_z, txt_l, txt_r))
    txt_1 = join(txt, txt_z, txt_l, txt_r)
    oth_1 = to_core(txt_1)
    pair_work = 2 * (width + 2 * width_s)
    grads = lambda *sizes: [((size * rows, width_s), f32) for size in sizes] + [((8, 128), f32)]
    imgs = [img, img_z, img_l]
    p_img, p_txt, p_oth, p_loss = call(
        run(near_tile_kernel, width_t), "near_tile", (*imgs, txt_1, oth_1), grads(3, 4, 4),
        flops=24 * rows * rows * pair_work,
    )
    txt_2 = join(txt_o, txt_zl)
    oth_2 = to_core(txt_2)
    imgs += [img_o, img_zl, img_r]
    p_img, p_txt, p_oth, p_loss = call(
        run(mid_tile_kernel, width_t), "mid_tile", (*imgs, txt_1, oth_1, txt_2, oth_2, p_img, p_txt, p_oth, p_loss),
        grads(6, 6, 6), limit=20, flops=48 * rows * rows * pair_work,
    )
    txt_zr, txt_zo, img_zo, img_zr, p_loss = hold((txt_zr, txt_zo, img_zo, img_zr, p_loss))
    txt_n = join(txt_zr, txt_zo)
    oth_n = to_core(txt_n)
    imgs += [img_zr, img_zo]
    texts = [txt_1, txt_2, oth_1, oth_2]
    coef_p, coef_t, loss = call(
        run(last_coef_kernel, width_t), "last_coef", (*imgs, *texts, txt_n, p_loss),
        [((12 * rows, 2 * rows), bf16), ((8 * rows, 2 * rows), bf16), ((8, 128), f32)], limit=24,
        flops=2 * (24 + 16) * rows * rows * width,
    )
    coef_u, loss = call(
        run(end_coef_kernel, width_t), "end_coef", (*imgs, oth_n, loss),
        [((8 * rows, 2 * rows), bf16), ((8, 128), f32)], flops=2 * 16 * rows * rows * width,
    )
    loss_core = to_core(loss)
    grad_work = 2 * (12 + 16) * rows * rows * width_s
    grad_o = call(
        run(text_grad_kernel, width_t, 1), "other_grad", (*imgs, coef_p, coef_u, p_oth),
        [((8 * rows, width_s), bf16)], flops=grad_work,
    )[0]
    grad_o, loss_core = hold((grad_o, loss_core))
    from_core = to_core(grad_o)
    loss, p_txt, p_img = hold((loss + loss_core, p_txt, p_img))
    loss_x = [to_x(loss, 1), to_x(loss, -1), to_x(loss, 2)]
    pair = 2 * rows
    sums = [((rows, width_s), f32), ((rows, width_s), bf16)]
    grad_t = call(
        run(text_grad_kernel, width_t, 0), "text_grad", (*imgs, coef_p, coef_t, p_txt),
        [((8 * rows, width_s), f32)], flops=grad_work,
    )[0]
    i0, i1, i2, i3, i4 = call(
        run(image_grad_kernel, width_t), "image_grad", (*texts, txt_n, oth_n, coef_p, coef_t, coef_u, p_img),
        [((pair, width_s), f32)] + [((pair, width_s), bf16)] * 2 + sums, flops=2 * grad_work,
    )
    loss_x, i0 = hold((loss_x, i0))
    loss = loss + loss_x[0] + loss_x[1] + loss_x[2]
    t0, t1, t2, t3, t4 = call(
        text_sum_kernel, "text_sum", (grad_t, from_core, loss),
        [((pair, width_s), f32)] + [((pair + 16, width_s), bf16)] * 2 + sums,
    )
    i4, i1, i2 = to_image_z(i4), to_x(i1, -1), to_x(i2, 1)
    loss_2 = to_y(loss, 2)
    t1, t2, t4 = to_y(t1, -1), to_y(t2, 1), to_text_z(t4)
    near, to_z, to_far = ((rows, width_s), f32), ((rows + 16, width_s), bf16), ((rows, width_s), bf16)
    img, img_z, img_x = call(ring_sum, "image_ring", (i0, i1, i2, i3, i4), [near, to_far, to_far])
    txt, txt_z, txt_x, img_z, loss = call(
        text_ring_kernel, "text_ring", (t0, t1, t2, t3, t4, loss, loss_2, img_z),
        [near, to_z, to_far, to_z, ((8, 128), f32)],
    )
    txt_x, img_x = to_y(txt_x, 2), to_x(img_x, 2)
    txt_z, img_z, loss_far = to_text_z(txt_z), to_image_z(img_z), to_far_z(loss)
    pairs = float(rows * lax.axis_size("dp") * lax.axis_size("blk"))
    image_grad, text_grad, loss = call(
        functools.partial(finish_kernel, 1.0 / (pairs * pairs)), "finish",
        (loss, loss_far, txt, txt_z, txt_x, img, img_z, img_x, student_image, student_text),
        [((rows, width_s), f32)] * 2 + [((1, 1), f32)],
        keep=False,
    )
    return (image_grad, text_grad, loss.reshape(()))


def solution(mesh):
    spec = P(AXES, None)
    return jax.shard_map(body, mesh=mesh, in_specs=(spec,) * 4, out_specs=(spec, spec, P()), check_vma=False)
```

```python
import functools
import itertools

import jax
import jax.numpy as jnp
from jax import lax
from jax.experimental import pallas as pl
from jax.experimental.pallas import tpu as pltpu
from jax.sharding import PartitionSpec as P

eps = 1e-06
scale = 10.0
bias = -2.0
AXES = ("dp", "blk")
f32, bf16 = jnp.float32, jnp.bfloat16

ZH, Y, C, X, ZL = 2, 4, 2, 4, 2
NT = (((1,), (1,)), ((), ()))
TN = (((0,), (0,)), ((), ()))


def place(zh, y, c, x, zl):
    return ((zh * Y + y) * C + c) * (X * ZL) + x * ZL + zl


def permute(value, move):
    pairs = [
        (place(*at), place(*move(*at)))
        for at in itertools.product(range(ZH), range(Y), range(C), range(X), range(ZL))
    ]
    return lax.ppermute(value, AXES, pairs)


def to_x(value, step):
    return permute(value, lambda zh, y, c, x, zl: (zh, y, c, (x + step) % X, zl))


def to_y(value, step):
    return permute(value, lambda zh, y, c, x, zl: (zh, (y + step) % Y, c, x, zl))


def flip_x(value, bits):
    return permute(value, lambda zh, y, c, x, zl: (zh, y, c, x ^ bits, zl))


def flip_y(value, bits):
    return permute(value, lambda zh, y, c, x, zl: (zh, y ^ bits, c, x, zl))


def to_core(value):
    return permute(value, lambda zh, y, c, x, zl: (zh, y, 1 - c, x, zl))


def to_image_z(value):
    return permute(value, lambda zh, y, c, x, zl: (zh, y, c, x, 1 - zl))


def to_text_z(value):
    return permute(value, lambda zh, y, c, x, zl: (1 - zh, y, c, x, 1 - zl))


def to_far_z(value):
    return permute(value, lambda zh, y, c, x, zl: (1 - zh, y, c, x, zl))


def call(kernel, name, args, outs, limit=16, far=(), keep=True, flops=0, scratch=()):
    vmem = pl.BlockSpec(memory_space=pltpu.VMEM)
    near = [
        pltpu.with_memory_space_constraint(v, pltpu.HBM if any(v is w for w in far) else pltpu.VMEM) for v in args
    ]
    shape_of = pltpu.VMEM if keep else jax.ShapeDtypeStruct
    return pl.pallas_call(
        kernel,
        out_shape=tuple(shape_of(shape, dtype) for shape, dtype in outs),
        in_specs=[vmem] * len(args),
        out_specs=(vmem,) * len(outs),
        scratch_shapes=[pltpu.VMEM(shape, dtype) for shape, dtype in scratch],
        compiler_params=pltpu.CompilerParams(vmem_limit_bytes=limit * 2**20),
        cost_estimate=pl.CostEstimate(
            flops=flops, transcendentals=0, bytes_accessed=sum(v.size * v.dtype.itemsize for v in args),
        ),
        name=name,
    )(*near)


def norm_of(wide):
    return jnp.sqrt(jnp.sum(wide * wide, axis=-1, keepdims=True) + eps)


def units_kernel(ti, si, tt, st, img, txt):
    for teach, stud, out in ((ti, si, img), (tt, st, txt)):
        wide = teach[...].astype(f32)
        split = wide.shape[1]
        out[:, :split] = (wide / norm_of(wide)).astype(bf16)
        wide = stud[...].astype(f32)
        out[:, split:] = (wide / norm_of(wide)).astype(bf16)


def tile_terms(cos_t, cos_s):
    half_s = cos_s * (0.5 * scale) + 0.5 * bias
    tanh_t = jnp.tanh(cos_t * (0.5 * scale) + 0.5 * bias)
    tanh_s = jnp.tanh(half_s)
    coef = ((tanh_s - tanh_t) * (0.5 * scale)).astype(bf16)
    left = 1.0 - tanh_s
    for _ in range(3):
        rows = left.shape[0] // 2
        left = left[:rows] * left[rows:]
    line = half_s + half_s * tanh_t
    fold = lambda v: jnp.sum(v.reshape(-1, 8, v.shape[1]), axis=0)
    loss = -(fold(jnp.log(left)) + fold(line))
    return coef, sum(loss[:, k:k + 128] for k in range(0, loss.shape[1], 128))


def stack(refs, cols):
    return jnp.concatenate([r[:, cols] for r in refs], axis=0)


def dot(a, b, dims=(((1,), (0,)), ((), ()))):
    return lax.dot_general(a, b, dims, preferred_element_type=f32)


def tile_blocks(left_t, left_s, right_t, right_s, size):
    coefs, total = [], jnp.zeros((8, 128), f32)
    for at in range(0, left_t.shape[0], size):
        part = slice(at, at + size)
        coef, loss = tile_terms(dot(left_t[part], right_t, NT), dot(left_s[part], right_s, NT))
        coefs.append(coef)
        total = total + loss
    return jnp.concatenate(coefs, axis=0), total


def near_tile_kernel(width_t, *refs):
    imgs, texts, (g_img, g_txt, g_oth, loss_ref) = refs[:3], refs[3:5], refs[5:]
    cols_t, cols_s = slice(0, width_t), slice(width_t, None)
    img_t, img_s, text_s = stack(imgs, cols_t), stack(imgs, cols_s), stack(texts, cols_s)
    coef, loss = tile_terms(dot(img_t, stack(texts, cols_t), NT), dot(img_s, text_s, NT))
    loss_ref[...] = loss
    g_img[...] = dot(coef, text_s)
    half = g_txt.shape[0]
    g_txt[...] = dot(coef[:, :half], img_s, TN)
    g_oth[...] = dot(coef[:, half:], img_s, TN)


def mid_tile_kernel(width_t, *refs):
    imgs, old, new, refs = refs[:6], refs[6:8], refs[8:10], refs[10:]
    p_img, p_txt, p_oth, p_loss, g_img, g_txt, g_oth, loss_ref = refs
    cols_t, cols_s = slice(0, width_t), slice(width_t, None)
    img_s, add_s = stack(imgs, cols_s), stack(imgs[3:], cols_s)
    old_s, new_s = stack(old, cols_s), stack(new, cols_s)
    coef_i, loss_i = tile_blocks(stack(imgs, cols_t), img_s, stack(new, cols_t), new_s, 256)
    coef_t, loss_t = tile_blocks(stack(old, cols_t), old_s, stack(imgs[3:], cols_t), add_s, 256)
    loss_ref[...] = p_loss[...] + loss_i + loss_t
    some, half, add = p_img.shape[0], p_txt.shape[0], new[0].shape[0]
    grad = dot(coef_i, new_s)
    g_img[:some, :] = p_img[...] + grad[:some]
    g_img[some:, :] = grad[some:] + dot(coef_t, old_s, TN)
    for n, (part, ref) in enumerate(((p_txt, g_txt), (p_oth, g_oth))):
        ref[:half, :] = part[...] + dot(coef_t[n * half:(n + 1) * half], add_s)
        ref[half:, :] = dot(coef_i[:, n * add:(n + 1) * add], img_s, TN)


def coef_blocks(width_t, rows, cols, out, size):
    cols_t, cols_s = slice(0, width_t), slice(width_t, None)
    right_t, right_s = stack(cols, cols_t), stack(cols, cols_s)
    left_t, left_s = stack(rows, cols_t), stack(rows, cols_s)
    total = jnp.zeros((8, 128), f32)
    for at in range(0, left_t.shape[0], size):
        part = slice(at, at + size)
        coef, loss = tile_terms(dot(left_t[part], right_t, NT), dot(left_s[part], right_s, NT))
        out[part, :] = coef
        total = total + loss
    return total


def last_coef_kernel(width_t, *refs):
    imgs, texts, last, (p_loss, coef_p, coef_t, loss_ref) = refs[:8], refs[8:12], refs[12], refs[13:]
    loss = coef_blocks(width_t, texts, imgs[6:], coef_p, 256) + coef_blocks(width_t, imgs, [last], coef_t, 256)
    loss_ref[...] = p_loss[...] + loss


def end_coef_kernel(width_t, *refs):
    imgs, (last, p_loss, coef_u, loss_ref) = refs[:8], refs[8:]
    loss_ref[...] = p_loss[...] + coef_blocks(width_t, imgs, [last], coef_u, 256)


def text_grad_kernel(width_t, core, *refs):
    imgs, (coef_p, coef_l, part, out) = refs[:8], refs[8:]
    cols_s = slice(width_t, None)
    most = part.shape[0]
    grad = part[...] + dot(coef_p[core * most:(core + 1) * most, :], stack(imgs[6:], cols_s))
    out[:most, :] = grad.astype(out.dtype)
    out[most:, :] = dot(coef_l[...], stack(imgs, cols_s), TN).astype(out.dtype)


def text_sum_kernel(own, from_core, loss, t0, t1, t2, t3, t4):
    at = lambda low, high: own[low:high, :] + from_core[low:high, :].astype(f32)
    t0[...] = at(0, 256)
    t1[0:128, :] = at(256, 384).astype(bf16)
    t1[128:256, :] = at(640, 768).astype(bf16)
    t2[0:128, :] = at(384, 512).astype(bf16)
    t2[128:256, :] = at(768, 896).astype(bf16)
    t3[...] = at(512, 640)
    t4[...] = at(896, 1024).astype(bf16)
    for ref in (t1, t2):
        put_pieces(ref, 256, loss[...])


def image_grad_kernel(width_t, *refs):
    texts, last_t, last_u = refs[:4], refs[4], refs[5]
    coef_p, coef_t, coef_u, part, i0, i1, i2, i3, i4 = refs[6:]
    cols_s = slice(width_t, None)
    most = part.shape[0]
    grad = dot(coef_t[...], last_t[:, cols_s]) + dot(coef_u[...], last_u[:, cols_s])
    early = part[...] + grad[:most]
    late = grad[most:] + dot(coef_p[...], stack(texts, cols_s), TN)
    i0[...] = early[0:256]
    i1[0:128, :] = early[256:384].astype(bf16)
    i1[128:256, :] = early[512:640].astype(bf16)
    i2[0:128, :] = early[640:768].astype(bf16)
    i2[128:256, :] = late[0:128].astype(bf16)
    i3[...] = early[384:512]
    i4[...] = late[128:256].astype(bf16)


def join(*parts):
    return jnp.concatenate(parts, axis=0)


def put_pieces(ref, row, value):
    ref[row:row + 16, :] = jnp.zeros((16, ref.shape[1]), bf16)
    first = value.astype(bf16)
    second = (value - first.astype(f32)).astype(bf16)
    third = (value - first.astype(f32) - second.astype(f32)).astype(bf16)
    ref[row:row + 16, 0:128] = jnp.concatenate([first, first], axis=0)
    ref[row:row + 16, 128:256] = jnp.concatenate([second, second], axis=0)
    ref[row:row + 16, 256:384] = jnp.concatenate([third, third], axis=0)


def get_pieces(ref, row):
    at = lambda k: ref[row:row + 16, k:k + 128].astype(f32)[:8]
    return at(0) + at(128) + at(256)


def ring_sum(own, one, two, far, from_z, near, to_z, to_far):
    rows = near.shape[0]
    total = own[...] + one[:2 * rows, :].astype(f32) + two[:2 * rows, :].astype(f32)
    near[...] = total[:rows]
    to_z[:rows, :] = total[rows:].astype(bf16)
    to_far[...] = (far[...] + from_z[...].astype(f32)).astype(bf16)


def text_ring_kernel(own, one, two, far, from_z, loss, loss_far, img_z, near, to_z, to_far, img_out, loss_out):
    rows = near.shape[0]
    loss_out[...] = loss[...] + loss_far[...] + get_pieces(one, 2 * rows) + get_pieces(two, 2 * rows)
    ring_sum(own, one, two, far, from_z, near, to_z, to_far)
    img_out[:rows, :] = img_z[...]
    for ref in (to_z, img_out):
        put_pieces(ref, rows, loss_out[...])


def finish_kernel(
    scale_loss, loss, loss_far, txt, txt_z, txt_x, img, img_z, img_x, si, st, img_out, txt_out, loss_out
):
    rows = txt.shape[0]
    for stud, near, far, ring, out in ((si, img, img_z, img_x, img_out), (st, txt, txt_z, txt_x, txt_out)):
        wide = stud[...].astype(f32)
        norm = norm_of(wide)
        unit = wide / norm
        grad = near[...] + far[:rows, :].astype(f32) + ring[...].astype(f32)
        out[...] = (grad - jnp.sum(grad * unit, axis=-1, keepdims=True) * unit) / norm
    total = (loss[...] + loss_far[...]) + (get_pieces(img_z, rows) + get_pieces(txt_z, rows))
    loss_out[...] = jnp.sum(total, keepdims=True) * scale_loss + jnp.log(2.0)


def body(teacher_image, teacher_text, student_image, student_text):
    rows, width_t = teacher_image.shape
    width_s = student_image.shape[1]
    width = width_t + width_s
    img, txt = call(
        units_kernel, "units", (teacher_image, student_image, teacher_text, student_text),
        [((rows, width), bf16)] * 2,
        far=(teacher_image, student_image, teacher_text, student_text),
    )

    hold = lax.optimization_barrier
    run = functools.partial
    txt_l, img_l, txt_z, img_z = to_y(txt, 1), to_x(img, 1), to_text_z(txt), to_image_z(img)
    txt_r = to_y(txt, -1)
    txt_o, img_o = to_y(txt_l, 1), to_x(img_l, 1)
    txt_zl, img_zl = to_text_z(hold((txt_l, txt_z))[0]), to_image_z(hold((img_l, img_z))[0])
    img_r = to_x(hold((img, img_z))[0], -1)
    txt_zo, img_zo = to_text_z(txt_o), to_image_z(img_o)
    txt_zr, img_zr = to_y(hold((txt_z, txt_zl))[0], -1), to_x(hold((img_z, img_zl))[0], -1)
    txt_o, img_o, txt_zl, img_zl, img_r, txt_z, txt_l, txt_r = hold((txt_o, img_o, txt_zl, img_zl, img_r, txt_z, txt_l, txt_r))
    txt_1 = join(txt, txt_z, txt_l, txt_r)
    oth_1 = to_core(txt_1)
    pair_work = 2 * (width + 2 * width_s)
    grads = lambda *sizes: [((size * rows, width_s), f32) for size in sizes] + [((8, 128), f32)]
    imgs = [img, img_z, img_l]
    p_img, p_txt, p_oth, p_loss = call(
        run(near_tile_kernel, width_t), "near_tile", (*imgs, txt_1, oth_1), grads(3, 4, 4),
        flops=24 * rows * rows * pair_work,
    )
    txt_2 = join(txt_o, txt_zl)
    oth_2 = to_core(txt_2)
    imgs += [img_o, img_zl, img_r]
    p_img, p_txt, p_oth, p_loss = call(
        run(mid_tile_kernel, width_t), "mid_tile", (*imgs, txt_1, oth_1, txt_2, oth_2, p_img, p_txt, p_oth, p_loss),
        grads(6, 6, 6), limit=20, flops=48 * rows * rows * pair_work,
    )
    txt_zr, txt_zo, img_zo, img_zr, p_loss = hold((txt_zr, txt_zo, img_zo, img_zr, p_loss))
    txt_n = join(txt_zr, txt_zo)
    oth_n = to_core(txt_n)
    imgs += [img_zr, img_zo]
    texts = [txt_1, txt_2, oth_1, oth_2]
    coef_p, coef_t, loss = call(
        run(last_coef_kernel, width_t), "last_coef", (*imgs, *texts, txt_n, p_loss),
        [((12 * rows, 2 * rows), bf16), ((8 * rows, 2 * rows), bf16), ((8, 128), f32)], limit=24,
        flops=2 * (24 + 16) * rows * rows * width,
    )
    coef_u, loss = call(
        run(end_coef_kernel, width_t), "end_coef", (*imgs, oth_n, loss),
        [((8 * rows, 2 * rows), bf16), ((8, 128), f32)], flops=2 * 16 * rows * rows * width,
    )
    loss_core = to_core(loss)
    grad_work = 2 * (12 + 16) * rows * rows * width_s
    grad_o = call(
        run(text_grad_kernel, width_t, 1), "other_grad", (*imgs, coef_p, coef_u, p_oth),
        [((8 * rows, width_s), bf16)], flops=grad_work,
    )[0]
    grad_o, loss_core = hold((grad_o, loss_core))
    from_core = to_core(grad_o)
    loss, p_txt, p_img = hold((loss + loss_core, p_txt, p_img))
    loss_x = [to_x(loss, 1), to_x(loss, -1), to_x(loss, 2)]
    pair = 2 * rows
    sums = [((rows, width_s), f32), ((rows, width_s), bf16)]
    grad_t = call(
        run(text_grad_kernel, width_t, 0), "text_grad", (*imgs, coef_p, coef_t, p_txt),
        [((8 * rows, width_s), f32)], flops=grad_work,
    )[0]
    i0, i1, i2, i3, i4 = call(
        run(image_grad_kernel, width_t), "image_grad", (*texts, txt_n, oth_n, coef_p, coef_t, coef_u, p_img),
        [((pair, width_s), f32)] + [((pair, width_s), bf16)] * 2 + sums, flops=2 * grad_work,
    )
    loss_x, i0 = hold((loss_x, i0))
    loss = loss + loss_x[0] + loss_x[1] + loss_x[2]
    t0, t1, t2, t3, t4 = call(
        text_sum_kernel, "text_sum", (grad_t, from_core, loss),
        [((pair, width_s), f32)] + [((pair + 16, width_s), bf16)] * 2 + sums,
    )
    i4, i1, i2 = to_image_z(i4), to_x(i1, -1), to_x(i2, 1)
    loss_2 = to_y(loss, 2)
    t1, t2, t4 = to_y(t1, -1), to_y(t2, 1), to_text_z(t4)
    near, to_z, to_far = ((rows, width_s), f32), ((rows + 16, width_s), bf16), ((rows, width_s), bf16)
    img, img_z, img_x = call(ring_sum, "image_ring", (i0, i1, i2, i3, i4), [near, to_far, to_far])
    txt, txt_z, txt_x, img_z, loss = call(
        text_ring_kernel, "text_ring", (t0, t1, t2, t3, t4, loss, loss_2, img_z),
        [near, to_z, to_far, to_z, ((8, 128), f32)],
    )
    txt_x, img_x = to_y(txt_x, 2), to_x(img_x, 2)
    txt_z, img_z, loss_far = to_text_z(txt_z), to_image_z(img_z), to_far_z(loss)
    pairs = float(rows * lax.axis_size("dp") * lax.axis_size("blk"))
    image_grad, text_grad, loss = call(
        functools.partial(finish_kernel, 1.0 / (pairs * pairs)), "finish",
        (loss, loss_far, txt, txt_z, txt_x, img, img_z, img_x, student_image, student_text),
        [((rows, width_s), f32)] * 2 + [((1, 1), f32)],
        keep=False,
    )
    return (image_grad, text_grad, loss.reshape(()))


def solution(mesh):
    spec = P(AXES, None)
    return jax.shard_map(body, mesh=mesh, in_specs=(spec,) * 4, out_specs=(spec, spec, P()), check_vma=False)
```
